32 devices in a mesh: dp: 4 (over y, core), expert: 8 (over z, x).
Axes of the slice: x: 2, y: 2, z: 4, core: 2. Of those that a mesh axis runs over, the one named last changes fastest.
Arguments:
- tokens: bfloat16 [384, 3584], P('dp', 'expert'), may hold values from -13 to 13
- routes: int32 [384, 8], replicated, may hold values from 0 to 31, all different within a row; in each aligned block of 96 rows (0 to 95, 96 to 191, ...) at most 32 rows name the same one
- gate_weight: bfloat16 [32, 3584, 2048], P('expert', None, 'dp'), may hold values from -0.09375 to 0.09375
- up_weight: bfloat16 [32, 3584, 2048], P('expert', None, 'dp'), may hold values from -0.09375 to 0.09375
- hidden_grad: bfloat16 [32, 4, 32, 2048], P('expert', None, None, 'dp'), may hold values from -40 to 40
- clip_limit: float32 [32], P('expert'), may hold values from 1 to 40
Outputs:
- hidden: bfloat16 [32, 4, 32, 2048], P('expert', None, None, 'dp')
- grad_gate: bfloat16 [32, 3584, 2048], P('expert', None, 'dp')
- grad_up: bfloat16 [32, 3584, 2048], P('expert', None, 'dp')
- token_grad: bfloat16 [384, 3584], P('dp', 'expert')
The draws below stay inside these ranges and needn't reach their ends.
Inputs may be any that keep to these rules, and one draw needn't show every extreme that they name: `routes`: each row names 8 different experts. In each aligned block of 96 rows (the tokens of one index of dp) no expert is named by more than 32 rows, a bound that some block reaches.
All inputs are finite; a program needn't handle non-finite values.
Results may differ from the reference program's by a relative error of at most 0.014.
Values may be sent and summed in bfloat16 or wider, within the bound.
A program may use at most 192 MiB of HBM per device.

```python
import math
import jax
import jax.numpy as jnp
import numpy as np
from jax import lax

D = 3584
F = 2048
TOP = 8
EXPERTS = 32
CAP = 32
TOK_DEV = 96
TOKENS = 384
HID = 512
N_DP = 4


def draw_tokens(key, part):
    key_values, key_scale = jax.random.split(key, 2)
    column_scale = 10.0 ** (jax.random.uniform(key_scale, (1, D), jnp.float32) - 0.5)
    values = jax.random.truncated_normal(key_values, -4.0, 4.0, (TOKENS, D), jnp.float32)
    return (values * column_scale).astype(jnp.bfloat16)


def draw_hidden_grad(key, part):
    key_values, key_columns, key_rows = jax.random.split(key, 3)
    unit_pos = (jnp.arange(F, dtype=jnp.float32) + 0.5) / F
    column_scale = 10.0 ** (jax.random.uniform(key_columns, (F,), jnp.float32) - 0.75) * 3.0 ** (unit_pos - 0.5)
    row_scale = 10.0 ** (jax.random.uniform(key_rows, (EXPERTS, N_DP, CAP, 1), jnp.float32) - 0.5)
    values = jax.random.truncated_normal(key_values, -4.0, 4.0, (EXPERTS, N_DP, CAP, F), jnp.float32)
    return (values * column_scale * row_scale).astype(jnp.bfloat16)


def levels(rng, shape, pieces, low, top_value):
    def one(dim, shards_of):
        steps = jax.random.uniform(jax.random.fold_in(jax.random.fold_in(rng, 6), dim), (shards_of,), jnp.float32, low / len(pieces), top_value / len(pieces))
        return jnp.repeat(jnp.exp(steps), shape[dim] // shards_of).reshape((-1,) + (1,) * (len(shape) - dim - 1))

    factor_of = one(*pieces[0])
    for cut in pieces[1:]:
        factor_of = factor_of * one(*cut)
    return factor_of


def assign_block(stream_key, own, number, rows, amount, top, bound, lean):
    order = jax.random.permutation(stream_key, amount)
    crowded, usual = load_shares(amount, rows * top, bound, lean, True), load_shares(amount, rows * top, bound, lean, False)
    places = jnp.arange(amount)

    def named(lengths, rotation):
        used = int((lengths > 0).sum())
        fixed = max(1, used // 4)
        shifted = fixed + (places - fixed + rotation * (used - fixed)) % max(1, amount - fixed)
        return jnp.zeros((amount,), jnp.int32).at[order[jnp.where(places < fixed, places, shifted)]].set(jnp.asarray(lengths, jnp.int32))

    lengths = jnp.where(number % 4 == 0, named(crowded, number // 4), named(usual, number - number // 4 - 1))
    mixed = jax.random.permutation(jax.random.fold_in(own, 3), amount)
    source_of, receiver = mixed[0:amount // 2 * 2:2], mixed[1:amount // 2 * 2:2]
    margin = jnp.minimum(lengths[source_of] - 1, bound - lengths[receiver]) // 2
    margin = jnp.where((source_of == order[0]) | (receiver == order[0]) | (lengths[receiver] == 0), 0, jnp.maximum(margin, 0))
    shifted = jax.random.randint(jax.random.fold_in(own, 4), (amount // 2,), 0, 1 << 20) % (margin + 1)
    lengths = lengths.at[source_of].add(-shifted).at[receiver].add(shifted)
    members = jnp.searchsorted(jnp.cumsum(lengths), jnp.arange(rows * top), side="right").astype(jnp.int32)
    grid = members.reshape(top, rows).T
    grid = grid[jax.random.permutation(jax.random.fold_in(own, 1), rows)]
    rotation = jax.random.randint(jax.random.fold_in(own, 2), (rows, 1), 0, top)
    return jnp.take_along_axis(grid, (jnp.arange(top)[None, :] + rotation) % top, axis=1)


def load_shares(count, total, most, skew, full):
    portions = [(1 << 20) // math.isqrt(rank ** skew) + 1 for rank in range(1, count + 1)]
    largest = most if full else min(most, max(-(-total // count), total * portions[0] // sum(portions)))
    least = 1 if total - largest >= count - 1 else 0
    counts, spare = [largest] + [least] * (count - 1), total - largest - least * (count - 1)
    while spare > 0:
        free = [i for i in range(1, count) if counts[i] < largest] or [i for i in range(1, count) if counts[i] < most]
        pool, remaining = sum([portions[i] for i in free]), spare
        for i in free:
            addition = min(most - counts[i], max(1, remaining * portions[i] // pool), spare)
            counts[i] = counts[i] + addition
            spare = spare - addition
    return np.array(counts)


def bell_draw(own_key, dims, width, bound, pieces=(), kind=jnp.bfloat16):
    result = jax.random.normal(own_key, dims, jnp.float32) * width
    if len(pieces) > 0:
        result = levels(own_key, dims, pieces, -0.22, 0.18) * result
    return jnp.clip(result, min=-bound, max=bound).astype(kind)


def setup_inputs(seed: int = 0) -> dict:
    arg_keys = jax.random.split(jax.random.key(seed), 7)
    tokens = draw_tokens(jax.random.fold_in(arg_keys[6], 71), 0)
    routes_keys = jax.random.split(jax.random.fold_in(arg_keys[1], 1), TOKENS // TOK_DEV)
    routes_turns = jax.random.permutation(jax.random.fold_in(arg_keys[1], 3), TOKENS // TOK_DEV)
    routes = jax.vmap(lambda own, number: assign_block(jax.random.fold_in(arg_keys[1], 2), own, number, TOK_DEV, EXPERTS, TOP, CAP, 1))(routes_keys, routes_turns).reshape((TOKENS, TOP))
    gate_weight = bell_draw(arg_keys[2], (EXPERTS, D, F), D ** -0.5, 0.09375, ((0, 8), (2, 4)))
    up_weight = bell_draw(arg_keys[3], (EXPERTS, D, F), D ** -0.5, 0.09375, ((0, 8), (2, 4)))
    hidden_grad = draw_hidden_grad(jax.random.fold_in(arg_keys[6], 71), 0)
    clip_limit = jnp.clip(jnp.exp(math.log(40.0) - 3.6888795 * jax.random.uniform(arg_keys[5], (EXPERTS,), jnp.float32) ** levels(arg_keys[5], (EXPERTS,), ((0, 8),), -0.2, 0.2)), 1.0, 40.0)
    return dict(tokens=tokens, routes=routes, gate_weight=gate_weight, up_weight=up_weight, hidden_grad=hidden_grad, clip_limit=clip_limit)


def slot_tables(block_routes):
    flat_routes = block_routes.reshape(-1)
    expert_ids = jnp.arange(EXPERTS, dtype=jnp.int32)
    onehot = (flat_routes[:, None] == expert_ids[None, :]).astype(jnp.int32)
    before = jnp.cumsum(onehot, axis=0) - onehot
    slot_ranks = lax.optimization_barrier(jnp.sum(before * onehot, axis=1)).astype(jnp.int32)
    owner_token = (jnp.arange(flat_routes.shape[0], dtype=jnp.int32) // TOP).astype(jnp.int32)
    token_of = jnp.zeros((EXPERTS, CAP), jnp.int32).at[flat_routes, slot_ranks].set(owner_token)
    occupied = jnp.zeros((EXPERTS, CAP), jnp.bool_).at[flat_routes, slot_ranks].set(True)
    return (slot_ranks.reshape(block_routes.shape), token_of, occupied)

def expert_pass(packed_item):
    dispatched, gate_w, up_w, grad_hidden, limit = packed_item
    gate_pre = jnp.dot(dispatched, gate_w, preferred_element_type=jnp.float32)
    up_pre = jnp.dot(dispatched, up_w, preferred_element_type=jnp.float32)
    sigma_gate = jax.nn.sigmoid(gate_pre)
    hidden = (gate_pre * sigma_gate * up_pre).astype(jnp.bfloat16)
    grad_float = grad_hidden.astype(jnp.float32)
    up_act = (grad_float * gate_pre * sigma_gate).astype(jnp.bfloat16)
    gate_act = (grad_float * up_pre * sigma_gate * (1.0 + gate_pre * (1.0 - sigma_gate))).astype(jnp.bfloat16)
    raw_gate = jnp.dot(dispatched.T, gate_act, preferred_element_type=jnp.float32)
    raw_up = jnp.dot(dispatched.T, up_act, preferred_element_type=jnp.float32)
    norm_sq = jnp.sum(raw_gate * raw_gate) + jnp.sum(raw_up * raw_up)
    root_mean = jnp.sqrt(norm_sq / (2.0 * D * F) + 1e-06)
    clip_scale = jnp.minimum(1.0, limit / root_mean)
    row_count = dispatched.shape[0]
    gate_blocks = gate_act.astype(jnp.float32).reshape(row_count, N_DP, HID)
    up_blocks = up_act.astype(jnp.float32).reshape(row_count, N_DP, HID)
    weight_gate = gate_w.astype(jnp.float32).reshape(D, N_DP, HID)
    weight_up = up_w.astype(jnp.float32).reshape(D, N_DP, HID)
    partial_value = jnp.einsum('rbh,dbh->rbd', gate_blocks, weight_gate, precision=lax.Precision.HIGHEST)
    partial_value = partial_value + jnp.einsum('rbh,dbh->rbd', up_blocks, weight_up, precision=lax.Precision.HIGHEST)
    partial_value = lax.optimization_barrier(partial_value.astype(jnp.bfloat16))
    slot_grad = lax.optimization_barrier(jnp.sum(partial_value.astype(jnp.float32), axis=1))
    grad_gate = (clip_scale * raw_gate).astype(jnp.bfloat16)
    grad_up = (clip_scale * raw_up).astype(jnp.bfloat16)
    return (hidden, grad_gate, grad_up, slot_grad)

def reference(tokens, routes, gate_weight, up_weight, hidden_grad, clip_limit):
    blocks = routes.reshape(N_DP, TOK_DEV, TOP)
    slot_ranks, token_of, occupied = jax.vmap(slot_tables)(blocks)
    offsets = (jnp.arange(N_DP, dtype=jnp.int32) * TOK_DEV)[:, None, None]
    gathered = jnp.where(occupied[..., None], tokens[(token_of + offsets).astype(jnp.int32)], jnp.zeros((), tokens.dtype))
    gathered = jnp.transpose(gathered, (1, 0, 2, 3)).reshape(EXPERTS, N_DP * CAP, D)
    grads_in = hidden_grad.reshape(EXPERTS, N_DP * CAP, F)
    hidden, grad_gate, grad_up, slot_grad = lax.map(expert_pass, (gathered, gate_weight, up_weight, grads_in, clip_limit))
    flat_slots = slot_grad.reshape(EXPERTS * N_DP * CAP, D)
    dp_ids = jnp.arange(N_DP, dtype=jnp.int32)[:, None, None]
    positions = ((blocks * N_DP + dp_ids) * CAP + slot_ranks).astype(jnp.int32)
    token_grad = lax.optimization_barrier(jnp.sum(flat_slots[positions], axis=2)).reshape(TOKENS, D).astype(jnp.bfloat16)
    return (hidden.reshape(EXPERTS, N_DP, CAP, F), grad_gate, grad_up, token_grad)
```

```python
import functools

import jax
import jax.numpy as jnp
from jax import lax
from jax.experimental import pallas as pl
from jax.experimental.pallas import tpu as pltpu
from jax.sharding import PartitionSpec as P


def slot_tables(block_routes, experts, capacity, top_count):
    flat_routes = block_routes.reshape(-1)
    expert_ids = jnp.arange(experts, dtype=jnp.int32)
    onehot = (flat_routes[:, None] == expert_ids[None, :]).astype(jnp.int32)
    before = jnp.cumsum(onehot, axis=0) - onehot
    slot_ranks = jnp.sum(before * onehot, axis=1)
    owner_token = jnp.arange(flat_routes.shape[0], dtype=jnp.int32) // top_count
    token_of = (
        jnp.zeros((experts, capacity), jnp.int32).at[flat_routes, slot_ranks].set(owner_token)
    )
    occupied = jnp.zeros((experts, capacity), jnp.bool_).at[flat_routes, slot_ranks].set(True)
    return (slot_ranks.reshape(block_routes.shape), token_of, occupied)


def expert_math(row_block, grad_block, gate_w, up_w):
    gate_pre = jnp.dot(row_block, gate_w, preferred_element_type=jnp.float32)
    up_pre = jnp.dot(row_block, up_w, preferred_element_type=jnp.float32)
    sigma_gate = jax.nn.sigmoid(gate_pre)
    hidden_rows = (gate_pre * sigma_gate * up_pre).astype(jnp.bfloat16)
    grad_float = grad_block.astype(jnp.float32)
    up_act = (grad_float * gate_pre * sigma_gate).astype(jnp.bfloat16)
    gate_act = (grad_float * up_pre * sigma_gate * (1.0 + gate_pre * (1.0 - sigma_gate))).astype(
        jnp.bfloat16
    )
    over_rows = (((0,), (0,)), ((), ()))
    over_units = (((1,), (1,)), ((), ()))
    raw_gate = lax.dot_general(row_block, gate_act, over_rows, preferred_element_type=jnp.float32)
    raw_up = lax.dot_general(row_block, up_act, over_rows, preferred_element_type=jnp.float32)
    partial_value = lax.dot_general(
        gate_act, gate_w, over_units, preferred_element_type=jnp.float32
    )
    partial_value = partial_value + lax.dot_general(
        up_act, up_w, over_units, preferred_element_type=jnp.float32
    )
    return (hidden_rows, raw_gate, raw_up, partial_value)


def plain_body(tokens, routes, gate_weight, up_weight, hidden_grad, clip_limit):
    dp_count = lax.axis_size("dp")
    expert_count = lax.axis_size("expert")
    local_experts = gate_weight.shape[0]
    experts = local_experts * expert_count
    capacity = hidden_grad.shape[2]
    hidden_units = gate_weight.shape[2]
    model_width = gate_weight.shape[1]
    top_count = routes.shape[1]
    tok_rows = tokens.shape[0]
    dp_index = lax.axis_index("dp")
    blocks = routes.reshape(dp_count, tok_rows, top_count)
    own_routes = lax.dynamic_index_in_dim(blocks, dp_index, 0, keepdims=False)
    slot_ranks, token_of, occupied = slot_tables(own_routes, experts, capacity, top_count)
    outgoing = jnp.where(occupied[:, :, None], tokens[token_of], jnp.zeros((), tokens.dtype))[
        :, None
    ]
    arrived = lax.all_to_all(outgoing, "expert", split_axis=0, concat_axis=3, tiled=True)
    gathered = lax.all_gather(arrived, "dp", axis=1, tiled=True)
    hidden_list = []
    gate_list = []
    up_list = []
    partial_list = []
    squares = []
    for expert_item in range(local_experts):
        row_block = gathered[expert_item].reshape(dp_count * capacity, model_width)
        grad_block = hidden_grad[expert_item].reshape(dp_count * capacity, hidden_units)
        hidden_rows, raw_gate, raw_up, partial_value = expert_math(
            row_block, grad_block, gate_weight[expert_item], up_weight[expert_item]
        )
        hidden_list.append(hidden_rows.reshape(dp_count, capacity, hidden_units))
        gate_list.append(raw_gate)
        up_list.append(raw_up)
        partial_list.append(partial_value.reshape(dp_count, capacity, model_width))
        squares.append(jnp.sum(raw_gate * raw_gate) + jnp.sum(raw_up * raw_up))
    totals = lax.psum(jnp.stack(squares), "dp")
    root_mean = jnp.sqrt(totals / (2.0 * model_width * hidden_units * dp_count) + 1e-06)
    clip_scale = jnp.minimum(1.0, clip_limit / root_mean)
    grad_gate = (clip_scale[:, None, None] * jnp.stack(gate_list)).astype(jnp.bfloat16)
    grad_up = (clip_scale[:, None, None] * jnp.stack(up_list)).astype(jnp.bfloat16)
    hidden = jnp.stack(hidden_list)
    partials = jnp.stack(partial_list)
    own_sums = lax.psum_scatter(
        partials.astype(jnp.bfloat16), "dp", scatter_dimension=1, tiled=True
    ).astype(jnp.float32)
    returned = lax.all_to_all(
        own_sums.astype(jnp.bfloat16), "expert", split_axis=3, concat_axis=0, tiled=True
    ).astype(own_sums.dtype)
    flat_back = returned.reshape(experts * capacity, -1)
    picked = flat_back[own_routes * capacity + slot_ranks]
    token_grad = jnp.sum(picked, axis=1).astype(jnp.bfloat16)
    return (hidden, grad_gate, grad_up, token_grad)


VMEM_LIMIT = 60 * 1024 * 1024
F32 = jnp.float32
BF16 = jnp.bfloat16
Z_COUNT = 4


def flip(bit, by):
    return bit + by - 2 * bit * by


class Place:
    def __init__(self):
        self.dp = lax.axis_index("dp")
        self.ex = lax.axis_index("expert")
        self.y, self.k = self.dp // 2, self.dp % 2
        self.z, self.x = self.ex // 2, self.ex % 2

    def z_at(self, j):
        return 2 * flip(self.z // 2, j // 2) + flip(self.z % 2, j % 2)

    def unit(self, core, s, f, j):
        xx = flip(self.x, f * (1 - core) + s * core)
        yy = flip(self.y, s * (1 - core) + f * core)
        return (2 * self.z_at(j) + xx) * 4 + 2 * yy + core

    def sibling(self):
        return (2 * self.y + 1 - self.k, self.ex)

    def second(self):
        return (2 * flip(self.y, 1 - self.k) + self.k, 2 * self.z + flip(self.x, self.k))

    def first(self):
        return (2 * flip(self.y, self.k) + self.k, 2 * self.z + flip(self.x, 1 - self.k))

    def along_z(self, j):
        return (self.dp, 2 * self.z_at(j) + self.x)

    def across(self):
        return (3 - self.dp, self.ex)

    def other_y(self):
        return (2 * (1 - self.y) + self.k, self.ex)

    def enter(self):
        barrier = pltpu.get_barrier_semaphore()
        partners = [self.sibling(), self.first(), self.second(), self.across()]
        partners += [self.along_z(j) for j in range(1, Z_COUNT)]
        for partner in partners:
            pl.semaphore_signal(
                barrier, inc=1, device_id=partner, device_id_type=pl.DeviceIdType.MESH
            )
        pl.semaphore_wait(barrier, len(partners))


def label(s, f, j):
    return s * 8 + f * 4 + j


class Gather:
    def __init__(self, place, units, send_sem, recv_sem):
        self.place, self.units = place, units
        self.send_sem, self.recv_sem = send_sem, recv_sem
        self.sent = []

    def copy(self, unit, device, send_index, recv_index):
        return pltpu.make_async_remote_copy(
            src_ref=self.units.at[unit],
            dst_ref=self.units.at[unit],
            send_sem=self.send_sem.at[send_index],
            recv_sem=self.recv_sem.at[recv_index],
            device_id=device,
            device_id_type=pl.DeviceIdType.MESH,
        )

    def send(self, unit, device, recv_index):
        copy = self.copy(unit, device, len(self.sent), recv_index)
        copy.start()
        self.sent.append(copy)

    def arrive(self, unit, recv_index):
        self.copy(unit, self.place.sibling(), 0, recv_index).wait_recv()

    def forward(self, s, f, j):
        place = self.place
        unit = place.unit(place.k, s, f, j)
        if (s, f, j) != (0, 0, 0):
            self.arrive(unit, label(s, f, j))
        if s == 0:
            self.send(unit, place.second(), label(1, f, j))
        if s == 0 and f == 0:
            self.send(unit, place.first(), label(0, 1, j))
        if (s, f, j) == (0, 0, 0):
            for j_to in range(1, Z_COUNT):
                self.send(unit, place.along_z(j_to), label(0, 0, j_to))
        self.send(unit, place.sibling(), 16 + label(s, f, j))

    def from_sibling(self, s, f, j):
        self.arrive(self.place.unit(1 - self.place.k, s, f, j), 16 + label(s, f, j))

    def finish(self):
        for copy in self.sent:
            copy.wait_send()


def gather_kernel(tokens_ref, units_ref, send_sem, recv_sem):
    place = Place()
    place.enter()
    units_ref[place.unit(place.k, 0, 0, 0)] = tokens_ref[...]
    gather = Gather(place, units_ref, send_sem, recv_sem)
    for j in range(Z_COUNT):
        gather.forward(0, 0, j)
        gather.forward(0, 1, j)
    for j in range(Z_COUNT):
        gather.forward(1, 0, j)
        gather.forward(1, 1, j)
    for j in range(Z_COUNT):
        for s in range(2):
            for f in range(2):
                gather.from_sibling(s, f, j)
    gather.finish()


def one_hot_rows(routes_ref, first_expert, experts, capacity, block_rows):
    tokens = routes_ref.shape[1]
    blocks = tokens // block_rows
    routes = routes_ref[...]
    masks = [
        jnp.sum((routes == first_expert + e).astype(F32), axis=0, keepdims=True)
        for e in range(experts)
    ]
    mask = jnp.concatenate(masks + [jnp.zeros((8 - experts, tokens), F32)], axis=0)
    earlier = lax.broadcasted_iota(jnp.int32, (tokens, tokens), 0)
    later = lax.broadcasted_iota(jnp.int32, (tokens, tokens), 1)
    block_start = jnp.zeros((tokens, tokens), jnp.int32)
    slot_start = jnp.zeros((8, tokens), jnp.int32)
    token = lax.broadcasted_iota(jnp.int32, (8, tokens), 1)
    for b in range(1, blocks):
        block_start = jnp.where(later >= b * block_rows, b * block_rows, block_start)
        slot_start = jnp.where(token >= b * block_rows, b * capacity, slot_start)
    counted = jnp.where((earlier < later) & (earlier >= block_start), 1.0, 0.0).astype(BF16)
    rank = jnp.dot(mask.astype(BF16), counted, preferred_element_type=F32)
    slot = jnp.where(mask > 0.5, rank + slot_start.astype(F32), -1.0)
    rows = lax.broadcasted_iota(jnp.int32, (blocks * capacity, tokens), 0).astype(F32)
    return jnp.concatenate(
        [jnp.where(rows == slot[e : e + 1], 1.0, 0.0).astype(BF16) for e in range(experts)], axis=0
    )


OVER_LANES = (((1,), (1,)), ((), ()))
OVER_ROWS = (((0,), (0,)), ((), ()))


def dot(a, b, dims=(((1,), (0,)), ((), ()))):
    return lax.dot_general(a, b, dims, preferred_element_type=F32)


def start_weights(gate_hbm, up_hbm, gate_v, up_v, weight_sem, chunk):
    width = gate_hbm.shape[1] // weight_sem.shape[1]
    rows = pl.ds(chunk * width, width)
    copies = [
        pltpu.make_async_copy(gate_hbm.at[:, rows], gate_v.at[:, rows], weight_sem.at[0, chunk]),
        pltpu.make_async_copy(up_hbm.at[:, rows], up_v.at[:, rows], weight_sem.at[1, chunk]),
    ]
    return copies


def activate(e, acc_ref, grad_ref, hidden_ref, act_ref):
    units = grad_ref.shape[2]
    gate_pre = acc_ref[e, :, :units]
    up_pre = acc_ref[e, :, units:]
    sigma = jax.nn.sigmoid(gate_pre)
    grad = grad_ref[e].astype(F32)
    hidden_ref[e] = (gate_pre * sigma * up_pre).astype(BF16)
    act_ref[e, :, units:] = (grad * gate_pre * sigma).astype(BF16)
    act_ref[e, :, :units] = (grad * up_pre * sigma * (1.0 + gate_pre * (1.0 - sigma))).astype(BF16)


def expert_kernel(
    routes_ref, units_ref, grad_ref, gate_hbm, up_hbm,
    hidden_ref, act_ref, rows_ref, sums_ref, square_ref,
    gate_v, up_v, onehot_ref, acc_ref, gram_ref, back_ref, weight_sem,
):
    experts, slots, units = grad_ref.shape
    chunks = rows_ref.shape[0]
    width = rows_ref.shape[2]
    d_count = units_ref.shape[0] // chunks
    block_rows = units_ref.shape[1]
    tokens = d_count * block_rows
    for chunk in range(chunks):
        for copy in start_weights(gate_hbm, up_hbm, gate_v, up_v, weight_sem, chunk):
            copy.start()
    first_expert = lax.axis_index("expert") * experts
    onehot = one_hot_rows(routes_ref, first_expert, experts, slots // d_count, block_rows)
    onehot_ref[...] = onehot
    back_ref[...] = onehot.T
    acc_ref[...] = jnp.zeros_like(acc_ref)
    gram_ref[...] = jnp.zeros_like(gram_ref)

    def forward(chunk, carry):
        for copy in start_weights(gate_hbm, up_hbm, gate_v, up_v, weight_sem, chunk):
            copy.wait()
        here = units_ref[pl.ds(chunk * d_count, d_count)].reshape(tokens, width)
        rows_ref[chunk] = dot(onehot_ref[...], here).astype(BF16)
        span = pl.ds(pl.multiple_of(chunk * width, 64), width)
        for e in range(experts):
            mine = rows_ref[chunk, e * slots : (e + 1) * slots]
            acc_ref[e, :, :units] += dot(mine, gate_v[e, span])
            acc_ref[e, :, units:] += dot(mine, up_v[e, span])
            gram_ref[e] += dot(mine, mine, OVER_LANES)
        return carry

    lax.fori_loop(0, chunks, forward, 0)
    squares = []
    for e in range(experts):
        activate(e, acc_ref, grad_ref, hidden_ref, act_ref)
        act = act_ref[e]
        product = dot(act, act, OVER_LANES) * gram_ref[e]
        squares.append(jnp.sum(jnp.sum(product, axis=0, keepdims=True), axis=1, keepdims=True))
    squares.append(jnp.zeros((8 - experts, 1), F32))
    square_ref[...] = jnp.broadcast_to(jnp.concatenate(squares, axis=0), square_ref.shape)

    def backward(chunk, carry):
        span = pl.ds(pl.multiple_of(chunk * width, 64), width)
        parts = []
        for e in range(experts):
            part = dot(act_ref[e, :, :units], gate_v[e, span], OVER_LANES)
            part = part + dot(act_ref[e, :, units:], up_v[e, span], OVER_LANES)
            parts.append(part.astype(BF16))
        total = dot(back_ref[...], jnp.concatenate(parts, axis=0))
        sums_ref[pl.ds(chunk * d_count, d_count)] = total.astype(BF16).reshape(
            d_count, block_rows, width
        )
        return carry

    lax.fori_loop(0, chunks, backward, 0)


class Scatter:
    def __init__(self, place, sums, work, buffers, send_sem, recv_sem):
        self.place, self.sums, self.work = place, sums, work
        self.buffers = buffers
        self.send_sem, self.recv_sem = send_sem, recv_sem
        self.sent = []

    def copy(self, src, dst, device, send_index, recv_index):
        return pltpu.make_async_remote_copy(
            src_ref=src,
            dst_ref=dst,
            send_sem=self.send_sem.at[send_index],
            recv_sem=self.recv_sem.at[recv_index],
            device_id=device,
            device_id_type=pl.DeviceIdType.MESH,
        )

    def send(self, src, slot, device):
        copy = self.copy(src, self.buffers.at[slot], device, len(self.sent), slot)
        copy.start()
        self.sent.append(copy)

    def take(self, slot):
        place = self.place
        landed = self.buffers.at[slot]
        self.copy(landed, landed, place.sibling(), 0, slot).wait_recv()
        return self.buffers[slot].astype(F32)

    def to_sibling(self, s, f, j):
        place = self.place
        unit = place.unit(1 - place.k, s, f, j)
        self.send(self.sums.at[unit], label(s, f, j), place.sibling())

    def collect(self, s, f, j):
        place = self.place
        total = self.sums[place.unit(place.k, s, f, j)].astype(F32)
        total = total + self.take(label(s, f, j))
        if s == 0:
            total = total + self.take(16 + f * 4 + j)
        if s == 0 and f == 0:
            total = total + self.take(24 + j)
        return total

    def pass_on(self, s, f, j):
        place = self.place
        held = label(s, f, j)
        self.work[held] = self.collect(s, f, j).astype(BF16)
        if s == 1:
            self.send(self.work.at[held], 16 + f * 4 + j, place.second())
        elif f == 1:
            self.send(self.work.at[held], 24 + j, place.first())
        else:
            self.send(self.work.at[held], 27 + j, place.along_z(j))

    def finish(self):
        for copy in self.sent:
            copy.wait_send()


def scatter_kernel(
    sums_ref, square_ref, token_ref, squares_ref,
    work, buffers, square_buf, send_sem, recv_sem, square_send, square_recv,
):
    place = Place()
    place.enter()
    scatter = Scatter(place, sums_ref, work, buffers, send_sem, recv_sem)
    others = [place.sibling(), place.other_y(), place.across()]
    square_copies = []
    for i, other in enumerate(others):
        copy = pltpu.make_async_remote_copy(
            src_ref=square_ref,
            dst_ref=square_buf.at[i],
            send_sem=square_send.at[i],
            recv_sem=square_recv.at[i],
            device_id=other,
            device_id_type=pl.DeviceIdType.MESH,
        )
        copy.start()
        square_copies.append(copy)
    order = [(s, f) for s in (1, 0) for f in (1, 0)]
    for s, f in order:
        for j in (1, 2, 3, 0):
            scatter.to_sibling(s, f, j)
    for s, f in order:
        for j in (1, 2, 3, 0):
            if (s, f, j) != (0, 0, 0):
                scatter.pass_on(s, f, j)
    total = scatter.collect(0, 0, 0)
    for j in range(1, Z_COUNT):
        total = total + scatter.take(27 + j)
    token_ref[...] = total.astype(BF16)
    squares = square_ref[...]
    for i, copy in enumerate(square_copies):
        copy.wait()
        squares = squares + square_buf[i]
    squares_ref[...] = squares
    scatter.finish()


def weight_grad_kernel(count, scale_ref, rows_ref, act_ref, gate_ref, up_ref):
    width = rows_ref.shape[2]
    units = gate_ref.shape[2]
    scale = scale_ref[pl.program_id(0)]
    for chunk in range(count):
        raw = dot(rows_ref[chunk], act_ref[0], OVER_ROWS) * scale
        gate_ref[0, chunk * width : (chunk + 1) * width] = raw[:, :units].astype(BF16)
        up_ref[0, chunk * width : (chunk + 1) * width] = raw[:, units:].astype(BF16)


def whole_vmem(count):
    return [pl.BlockSpec(memory_space=pltpu.VMEM)] * count


def kernel_body(tokens, routes, gate_weight, up_weight, hidden_grad, clip_limit):
    chunks = lax.axis_size("expert")
    d_count = lax.axis_size("dp")
    experts, model_width, hidden_units = gate_weight.shape
    block_rows, width = tokens.shape
    capacity = hidden_grad.shape[2]
    slots = d_count * capacity
    all_units = chunks * d_count
    token_rows = d_count * block_rows
    units = pl.pallas_call(
        gather_kernel,
        out_shape=jax.ShapeDtypeStruct((all_units, block_rows, width), BF16),
        in_specs=whole_vmem(1),
        out_specs=whole_vmem(1)[0],
        scratch_shapes=[pltpu.SemaphoreType.DMA((31,)), pltpu.SemaphoreType.DMA((32,))],
        compiler_params=pltpu.CompilerParams(
            collective_id=0, has_side_effects=True, vmem_limit_bytes=VMEM_LIMIT
        ),
        name="gather_tokens",
    )(tokens)
    hidden, act, rows, sums, square = pl.pallas_call(
        expert_kernel,
        out_shape=[
            jax.ShapeDtypeStruct((experts, slots, hidden_units), BF16),
            jax.ShapeDtypeStruct((experts, slots, 2 * hidden_units), BF16),
            jax.ShapeDtypeStruct((chunks, experts * slots, width), BF16),
            jax.ShapeDtypeStruct((all_units, block_rows, width), BF16),
            jax.ShapeDtypeStruct((8, 128), F32),
        ],
        in_specs=whole_vmem(3) + [pl.BlockSpec(memory_space=pl.ANY)] * 2,
        out_specs=whole_vmem(5),
        scratch_shapes=[
            pltpu.VMEM((experts, model_width, hidden_units), BF16),
            pltpu.VMEM((experts, model_width, hidden_units), BF16),
            pltpu.VMEM((experts * slots, token_rows), BF16),
            pltpu.VMEM((experts, slots, 2 * hidden_units), F32),
            pltpu.VMEM((experts, slots, slots), F32),
            pltpu.VMEM((token_rows, experts * slots), BF16),
            pltpu.SemaphoreType.DMA((2, chunks)),
        ],
        compiler_params=pltpu.CompilerParams(vmem_limit_bytes=VMEM_LIMIT),
        name="experts",
    )(routes.T, units, hidden_grad.reshape(experts, slots, hidden_units), gate_weight, up_weight)
    token_grad, squares = pl.pallas_call(
        scatter_kernel,
        out_shape=[
            jax.ShapeDtypeStruct((block_rows, width), BF16),
            jax.ShapeDtypeStruct((8, 128), F32),
        ],
        in_specs=whole_vmem(2),
        out_specs=whole_vmem(2),
        scratch_shapes=[
            pltpu.VMEM((16, block_rows, width), BF16),
            pltpu.VMEM((31, block_rows, width), BF16),
            pltpu.VMEM((3, 8, 128), F32),
            pltpu.SemaphoreType.DMA((31,)),
            pltpu.SemaphoreType.DMA((31,)),
            pltpu.SemaphoreType.DMA((3,)),
            pltpu.SemaphoreType.DMA((3,)),
        ],
        compiler_params=pltpu.CompilerParams(
            collective_id=1, has_side_effects=True, vmem_limit_bytes=VMEM_LIMIT
        ),
        name="scatter_grads",
    )(sums, square)
    grad_gate, grad_up = weight_grads(rows, act, squares, clip_limit, gate_weight.shape, d_count)
    return (hidden.reshape(hidden_grad.shape), grad_gate, grad_up, token_grad)


def weight_grads(rows, act, squares, clip_limit, shape, d_count):
    experts, model_width, hidden_units = shape
    chunks, _, width = rows.shape
    slots = act.shape[1]
    mean = squares[:experts, 0] / (2.0 * model_width * hidden_units * d_count)
    scale = jnp.minimum(1.0, clip_limit / jnp.sqrt(mean + 1e-06))
    halves = 2
    count = chunks // halves
    out_block = pl.BlockSpec((1, count * width, hidden_units), lambda e, h: (e, h, 0))
    return pl.pallas_call(
        functools.partial(weight_grad_kernel, count),
        grid=(experts, halves),
        out_shape=[jax.ShapeDtypeStruct(shape, BF16)] * 2,
        in_specs=[
            pl.BlockSpec(memory_space=pltpu.SMEM),
            pl.BlockSpec((count, slots, width), lambda e, h: (h, e, 0)),
            pl.BlockSpec((1, slots, 2 * hidden_units), lambda e, h: (e, 0, 0)),
        ],
        out_specs=[out_block, out_block],
        compiler_params=pltpu.CompilerParams(vmem_limit_bytes=VMEM_LIMIT),
        name="weight_grads",
    )(scale, rows, act)


def solution(mesh):
    placed = (
        P("dp", "expert"),
        P(),
        P("expert", None, "dp"),
        P("expert", None, "dp"),
        P("expert", None, None, "dp"),
        P("expert"),
    )
    fits = mesh.shape["dp"] == 4 and mesh.shape["expert"] == 2 * Z_COUNT
    return jax.shard_map(
        kernel_body if fits else plain_body,
        mesh=mesh,
        in_specs=placed,
        out_specs=(
            P("expert", None, None, "dp"),
            P("expert", None, "dp"),
            P("expert", None, "dp"),
            P("dp", "expert"),
        ),
        check_vma=False,
    )
```

```python
import functools

import jax
import jax.numpy as jnp
from jax import lax
from jax.experimental import pallas as pl
from jax.experimental.pallas import tpu as pltpu
from jax.sharding import PartitionSpec as P


def slot_tables(block_routes, experts, capacity, top_count):
    flat_routes = block_routes.reshape(-1)
    expert_ids = jnp.arange(experts, dtype=jnp.int32)
    onehot = (flat_routes[:, None] == expert_ids[None, :]).astype(jnp.int32)
    before = jnp.cumsum(onehot, axis=0) - onehot
    slot_ranks = jnp.sum(before * onehot, axis=1)
    owner_token = jnp.arange(flat_routes.shape[0], dtype=jnp.int32) // top_count
    token_of = (
        jnp.zeros((experts, capacity), jnp.int32).at[flat_routes, slot_ranks].set(owner_token)
    )
    occupied = jnp.zeros((experts, capacity), jnp.bool_).at[flat_routes, slot_ranks].set(True)
    return (slot_ranks.reshape(block_routes.shape), token_of, occupied)


def expert_math(row_block, grad_block, gate_w, up_w):
    gate_pre = jnp.dot(row_block, gate_w, preferred_element_type=jnp.float32)
    up_pre = jnp.dot(row_block, up_w, preferred_element_type=jnp.float32)
    sigma_gate = jax.nn.sigmoid(gate_pre)
    hidden_rows = (gate_pre * sigma_gate * up_pre).astype(jnp.bfloat16)
    grad_float = grad_block.astype(jnp.float32)
    up_act = (grad_float * gate_pre * sigma_gate).astype(jnp.bfloat16)
    gate_act = (grad_float * up_pre * sigma_gate * (1.0 + gate_pre * (1.0 - sigma_gate))).astype(
        jnp.bfloat16
    )
    over_rows = (((0,), (0,)), ((), ()))
    over_units = (((1,), (1,)), ((), ()))
    raw_gate = lax.dot_general(row_block, gate_act, over_rows, preferred_element_type=jnp.float32)
    raw_up = lax.dot_general(row_block, up_act, over_rows, preferred_element_type=jnp.float32)
    partial_value = lax.dot_general(
        gate_act, gate_w, over_units, preferred_element_type=jnp.float32
    )
    partial_value = partial_value + lax.dot_general(
        up_act, up_w, over_units, preferred_element_type=jnp.float32
    )
    return (hidden_rows, raw_gate, raw_up, partial_value)


def plain_body(tokens, routes, gate_weight, up_weight, hidden_grad, clip_limit):
    dp_count = lax.axis_size("dp")
    expert_count = lax.axis_size("expert")
    local_experts = gate_weight.shape[0]
    experts = local_experts * expert_count
    capacity = hidden_grad.shape[2]
    hidden_units = gate_weight.shape[2]
    model_width = gate_weight.shape[1]
    top_count = routes.shape[1]
    tok_rows = tokens.shape[0]
    dp_index = lax.axis_index("dp")
    blocks = routes.reshape(dp_count, tok_rows, top_count)
    own_routes = lax.dynamic_index_in_dim(blocks, dp_index, 0, keepdims=False)
    slot_ranks, token_of, occupied = slot_tables(own_routes, experts, capacity, top_count)
    outgoing = jnp.where(occupied[:, :, None], tokens[token_of], jnp.zeros((), tokens.dtype))[
        :, None
    ]
    arrived = lax.all_to_all(outgoing, "expert", split_axis=0, concat_axis=3, tiled=True)
    gathered = lax.all_gather(arrived, "dp", axis=1, tiled=True)
    hidden_list = []
    gate_list = []
    up_list = []
    partial_list = []
    squares = []
    for expert_item in range(local_experts):
        row_block = gathered[expert_item].reshape(dp_count * capacity, model_width)
        grad_block = hidden_grad[expert_item].reshape(dp_count * capacity, hidden_units)
        hidden_rows, raw_gate, raw_up, partial_value = expert_math(
            row_block, grad_block, gate_weight[expert_item], up_weight[expert_item]
        )
        hidden_list.append(hidden_rows.reshape(dp_count, capacity, hidden_units))
        gate_list.append(raw_gate)
        up_list.append(raw_up)
        partial_list.append(partial_value.reshape(dp_count, capacity, model_width))
        squares.append(jnp.sum(raw_gate * raw_gate) + jnp.sum(raw_up * raw_up))
    totals = lax.psum(jnp.stack(squares), "dp")
    root_mean = jnp.sqrt(totals / (2.0 * model_width * hidden_units * dp_count) + 1e-06)
    clip_scale = jnp.minimum(1.0, clip_limit / root_mean)
    grad_gate = (clip_scale[:, None, None] * jnp.stack(gate_list)).astype(jnp.bfloat16)
    grad_up = (clip_scale[:, None, None] * jnp.stack(up_list)).astype(jnp.bfloat16)
    hidden = jnp.stack(hidden_list)
    partials = jnp.stack(partial_list)
    own_sums = lax.psum_scatter(
        partials.astype(jnp.bfloat16), "dp", scatter_dimension=1, tiled=True
    ).astype(jnp.float32)
    returned = lax.all_to_all(
        own_sums.astype(jnp.bfloat16), "expert", split_axis=3, concat_axis=0, tiled=True
    ).astype(own_sums.dtype)
    flat_back = returned.reshape(experts * capacity, -1)
    picked = flat_back[own_routes * capacity + slot_ranks]
    token_grad = jnp.sum(picked, axis=1).astype(jnp.bfloat16)
    return (hidden, grad_gate, grad_up, token_grad)


VMEM_LIMIT = 60 * 1024 * 1024
F32 = jnp.float32
BF16 = jnp.bfloat16
Z_COUNT = 4


def flip(bit, by):
    return bit + by - 2 * bit * by


class Place:
    def __init__(self):
        self.dp = lax.axis_index("dp")
        self.ex = lax.axis_index("expert")
        self.y, self.k = self.dp // 2, self.dp % 2
        self.z, self.x = self.ex // 2, self.ex % 2

    def z_at(self, j):
        return 2 * flip(self.z // 2, j // 2) + flip(self.z % 2, j % 2)

    def unit(self, core, s, f, j):
        xx = flip(self.x, f * (1 - core) + s * core)
        yy = flip(self.y, s * (1 - core) + f * core)
        return (2 * self.z_at(j) + xx) * 4 + 2 * yy + core

    def sibling(self):
        return (2 * self.y + 1 - self.k, self.ex)

    def second(self):
        return (2 * flip(self.y, 1 - self.k) + self.k, 2 * self.z + flip(self.x, self.k))

    def first(self):
        return (2 * flip(self.y, self.k) + self.k, 2 * self.z + flip(self.x, 1 - self.k))

    def along_z(self, j):
        return (self.dp, 2 * self.z_at(j) + self.x)

    def across(self):
        return (3 - self.dp, self.ex)

    def other_y(self):
        return (2 * (1 - self.y) + self.k, self.ex)

    def enter(self):
        barrier = pltpu.get_barrier_semaphore()
        partners = [self.sibling(), self.first(), self.second(), self.across()]
        partners += [self.along_z(j) for j in range(1, Z_COUNT)]
        for partner in partners:
            pl.semaphore_signal(
                barrier, inc=1, device_id=partner, device_id_type=pl.DeviceIdType.MESH
            )
        pl.semaphore_wait(barrier, len(partners))


def label(s, f, j):
    return s * 8 + f * 4 + j


class Gather:
    def __init__(self, place, units, send_sem, recv_sem):
        self.place, self.units = place, units
        self.send_sem, self.recv_sem = send_sem, recv_sem

    def copy(self, unit, device, send_index, recv_index):
        return pltpu.make_async_remote_copy(
            src_ref=self.units.at[unit],
            dst_ref=self.units.at[unit],
            send_sem=self.send_sem.at[send_index],
            recv_sem=self.recv_sem.at[recv_index],
            device_id=device,
            device_id_type=pl.DeviceIdType.MESH,
        )

    def arrive(self, unit, recv_index):
        self.copy(unit, self.place.sibling(), 0, recv_index).wait_recv()

    def forward(self, s, f, j, own=False):
        place = self.place
        unit = place.unit(place.k, s, f, j)
        if not own:
            self.arrive(unit, label(s, f, j))
        if s == 0:
            self.copy(unit, place.second(), f * 4 + j, label(1, f, j)).start()
        if s == 0 and f == 0:
            self.copy(unit, place.first(), 8 + j, label(0, 1, j)).start()
        if own:
            for to in range(1, Z_COUNT):
                self.copy(unit, place.along_z(to), 11 + to, label(0, 0, to)).start()
        held = label(s, f, j)
        self.copy(unit, place.sibling(), 15 + held, 16 + held).start()

    def from_sibling(self, xf, yf, j):
        core = 1 - self.place.k
        s, f = xf * core + yf * (1 - core), xf * (1 - core) + yf * core
        self.arrive(self.place.unit(core, s, f, j), 16 + label(s, f, j))

    def finish(self):
        for i in range(31):
            self.copy(self.place.unit(self.place.k, 0, 0, 0), self.place.sibling(), i, 0).wait_send()


def one_hot_rows(routes_ref, first_expert, experts, capacity, block_rows):
    tokens = routes_ref.shape[1]
    blocks = tokens // block_rows
    routes = routes_ref[...]
    masks = [
        jnp.sum((routes == first_expert + e).astype(F32), axis=0, keepdims=True)
        for e in range(experts)
    ]
    mask = jnp.concatenate(masks + [jnp.zeros((8 - experts, tokens), F32)], axis=0)
    earlier = lax.broadcasted_iota(jnp.int32, (tokens, tokens), 0)
    later = lax.broadcasted_iota(jnp.int32, (tokens, tokens), 1)
    block_start = jnp.zeros((tokens, tokens), jnp.int32)
    slot_start = jnp.zeros((8, tokens), jnp.int32)
    token = lax.broadcasted_iota(jnp.int32, (8, tokens), 1)
    for b in range(1, blocks):
        block_start = jnp.where(later >= b * block_rows, b * block_rows, block_start)
        slot_start = jnp.where(token >= b * block_rows, b * capacity, slot_start)
    counted = jnp.where((earlier < later) & (earlier >= block_start), 1.0, 0.0).astype(BF16)
    rank = jnp.dot(mask.astype(BF16), counted, preferred_element_type=F32)
    slot = jnp.where(mask > 0.5, rank + slot_start.astype(F32), -1.0)
    rows = lax.broadcasted_iota(jnp.int32, (blocks * capacity, tokens), 0).astype(F32)
    return jnp.concatenate(
        [jnp.where(rows == slot[e : e + 1], 1.0, 0.0).astype(BF16) for e in range(experts)], axis=0
    )


OVER_LANES = (((1,), (1,)), ((), ()))
OVER_ROWS = (((0,), (0,)), ((), ()))


def dot(a, b, dims=(((1,), (0,)), ((), ()))):
    return lax.dot_general(a, b, dims, preferred_element_type=F32)


def start_weights(gate_hbm, up_hbm, gate_v, up_v, weight_sem, chunk):
    width = gate_hbm.shape[1] // weight_sem.shape[1]
    rows = pl.ds(chunk * width, width)
    copies = [
        pltpu.make_async_copy(gate_hbm.at[:, rows], gate_v.at[:, rows], weight_sem.at[0, chunk]),
        pltpu.make_async_copy(up_hbm.at[:, rows], up_v.at[:, rows], weight_sem.at[1, chunk]),
    ]
    return copies


def activate(e, acc_ref, grad_ref, hidden_ref, act_ref):
    units = grad_ref.shape[2]
    gate_pre = acc_ref[e, :, :units]
    up_pre = acc_ref[e, :, units:]
    sigma = jax.nn.sigmoid(gate_pre)
    grad = grad_ref[e].astype(F32)
    hidden_ref[e] = (gate_pre * sigma * up_pre).astype(BF16)
    act_ref[e, :, units:] = (grad * gate_pre * sigma).astype(BF16)
    act_ref[e, :, :units] = (grad * up_pre * sigma * (1.0 + gate_pre * (1.0 - sigma))).astype(BF16)


class Scatter:
    def __init__(self, place, sums, work, buffers, send_sem, recv_sem):
        self.place, self.sums, self.work = place, sums, work
        self.buffers = buffers
        self.send_sem, self.recv_sem = send_sem, recv_sem

    def copy(self, src, slot, device):
        return pltpu.make_async_remote_copy(
            src_ref=src,
            dst_ref=self.buffers.at[slot],
            send_sem=self.send_sem.at[slot],
            recv_sem=self.recv_sem.at[slot],
            device_id=device,
            device_id_type=pl.DeviceIdType.MESH,
        )

    def take(self, slot):
        self.copy(self.buffers.at[slot], slot, self.place.sibling()).wait_recv()
        return self.buffers[slot].astype(F32)

    def to_sibling(self, xf, j):
        place = self.place
        core = 1 - place.k
        for yf in range(2):
            s, f = xf * core + yf * (1 - core), xf * (1 - core) + yf * core
            unit = place.unit(core, s, f, j)
            self.copy(self.sums.at[unit], label(s, f, j), place.sibling()).start()

    def collect(self, s, f, j):
        place = self.place
        total = self.sums[place.unit(place.k, s, f, j)].astype(F32)
        total = total + self.take(label(s, f, j))
        if s == 0:
            total = total + self.take(16 + f * 4 + j)
        if s == 0 and f == 0:
            total = total + self.take(24 + j)
        return total

    def pass_on(self, s, f, j):
        place = self.place
        held = label(s, f, j)
        self.work[held] = self.collect(s, f, j).astype(BF16)
        if s == 1:
            self.copy(self.work.at[held], 16 + f * 4 + j, place.second()).start()
        else:
            self.copy(self.work.at[held], 24 + j, place.first()).start()

    def finish(self):
        for slot in range(28):
            self.copy(self.buffers.at[slot], slot, self.place.sibling()).wait_send()


def expert_kernel(
    tokens_ref, routes_ref, grad_ref, limit_ref, gate_hbm, up_hbm,
    hidden_ref, act_ref, rows_ref, scale_ref, total_ref,
    units_ref, sums_ref, gate_v, up_v, onehot_ref, acc_ref, gram_ref, back_ref,
    work, buffers, square_ref, square_buf,
    weight_sem, gather_send, gather_recv, scatter_send, scatter_recv, square_send, square_recv,
):
    experts, slots, units = grad_ref.shape
    chunks = rows_ref.shape[0]
    width = rows_ref.shape[2]
    d_count = units_ref.shape[0] // chunks
    block_rows = units_ref.shape[1]
    tokens = d_count * block_rows
    place = Place()

    def chunk_at(xf, j):
        return 2 * place.z_at(j) + flip(place.x, xf)

    def weights(chunk):
        return start_weights(gate_hbm, up_hbm, gate_v, up_v, weight_sem, chunk)

    for j in range(Z_COUNT):
        for xf in range(2):
            for copy in weights(chunk_at(xf, j)):
                copy.start()
    units_ref[place.unit(place.k, 0, 0, 0)] = tokens_ref[...]
    place.enter()
    gather = Gather(place, units_ref, gather_send, gather_recv)
    gather.forward(0, 0, 0, own=True)

    first_expert = place.ex * experts
    onehot = one_hot_rows(routes_ref, first_expert, experts, slots // d_count, block_rows)
    onehot_ref[...] = onehot
    back_ref[...] = onehot.T
    acc_ref[...] = jnp.zeros_like(acc_ref)
    gram_ref[...] = jnp.zeros_like(gram_ref)

    for j in range(Z_COUNT):
        if j > 0:
            gather.forward(0, 0, j)
        gather.forward(0, 1, j)
    gather.forward(1, 0, 0)
    gather.forward(1, 1, 0)

    def multiply(xf, j):
        chunk = chunk_at(xf, j)
        gather.from_sibling(xf, 0, j)
        gather.from_sibling(xf, 1, j)
        for copy in weights(chunk):
            copy.wait()
        here = units_ref[pl.ds(chunk * d_count, d_count)].reshape(tokens, width)
        rows_ref[chunk] = dot(onehot_ref[...], here).astype(BF16)
        span = pl.ds(pl.multiple_of(chunk * width, 64), width)
        for e in range(experts):
            mine = rows_ref[chunk, e * slots : (e + 1) * slots]
            acc_ref[e, :, :units] += dot(mine, gate_v[e, span])
            acc_ref[e, :, units:] += dot(mine, up_v[e, span])
            gram_ref[e] += dot(mine, mine, OVER_LANES)

    def forward(j, carry):
        multiply(0, j)

        @pl.when(j < Z_COUNT - 1)
        def _():
            gather.forward(1, 0, j + 1)
            gather.forward(1, 1, j + 1)

        multiply(1, j)
        return carry

    lax.fori_loop(0, Z_COUNT, forward, 0)
    squares = []
    for e in range(experts):
        activate(e, acc_ref, grad_ref, hidden_ref, act_ref)
        act = act_ref[e]
        product = dot(act, act, OVER_LANES) * gram_ref[e]
        squares.append(jnp.sum(jnp.sum(product, axis=0, keepdims=True), axis=1, keepdims=True))
    squares.append(jnp.zeros((8 - experts, 1), F32))
    square_ref[...] = jnp.broadcast_to(jnp.concatenate(squares, axis=0), square_ref.shape)
    square_copies = []
    for i, other in enumerate([place.sibling(), place.other_y(), place.across()]):
        copy = pltpu.make_async_remote_copy(
            src_ref=square_ref,
            dst_ref=square_buf.at[i],
            send_sem=square_send.at[i],
            recv_sem=square_recv.at[i],
            device_id=other,
            device_id_type=pl.DeviceIdType.MESH,
        )
        copy.start()
        square_copies.append(copy)

    scatter = Scatter(place, sums_ref, work, buffers, scatter_send, scatter_recv)

    def divide(xf, j):
        chunk = chunk_at(xf, j)
        span = pl.ds(pl.multiple_of(chunk * width, 64), width)
        parts = []
        for e in range(experts):
            part = dot(act_ref[e, :, :units], gate_v[e, span], OVER_LANES)
            part = part + dot(act_ref[e, :, units:], up_v[e, span], OVER_LANES)
            parts.append(part.astype(BF16))
        total = dot(back_ref[...], jnp.concatenate(parts, axis=0))
        sums_ref[pl.ds(chunk * d_count, d_count)] = total.astype(BF16).reshape(
            d_count, block_rows, width
        )
        scatter.to_sibling(xf, j)

    def far(j):
        scatter.pass_on(1, 1, j)

        @pl.when(place.k == 1)
        def _():
            scatter.pass_on(1, 0, j)

    def near(j):
        @pl.when(place.k == 0)
        def _():
            scatter.pass_on(1, 0, j)

        scatter.pass_on(0, 1, j)

    def backward_far(i, carry):
        divide(1, (i + 1) % Z_COUNT)

        @pl.when(i > 0)
        def _():
            far(i)

        return carry

    def backward_near(i, carry):
        divide(0, (i + 1) % Z_COUNT)

        @pl.when(i > 0)
        def _():
            near(i)

        @pl.when(i == 0)
        def _():
            far(0)

        return carry

    lax.fori_loop(0, Z_COUNT, backward_far, 0)
    lax.fori_loop(0, Z_COUNT, backward_near, 0)
    near(0)
    total_squares = square_ref[...]
    for i, copy in enumerate(square_copies):
        copy.wait()
        total_squares = total_squares + square_buf[i]
    mean = total_squares / (2.0 * chunks * width * units * d_count)
    scale = jnp.minimum(1.0, limit_ref[...] / jnp.sqrt(mean + 1e-06))
    for e in range(experts):
        scale_ref[e] = scale[e : e + 1]
    for j in (1, 2, 3, 0):
        total_ref[j] = scatter.collect(0, 0, j).astype(BF16)
    gather.finish()
    scatter.finish()


def weight_grad_kernel(count, scale_ref, rows_ref, act_ref, hidden_ref, gate_ref, up_ref, out_ref):
    width = rows_ref.shape[2]
    units = gate_ref.shape[2]
    scale = scale_ref[0, 0:1, 0:1]
    out_ref[...] = hidden_ref[...]
    for chunk in range(count):
        raw = dot(rows_ref[chunk], act_ref[0], OVER_ROWS) * scale
        gate_ref[0, chunk * width : (chunk + 1) * width] = raw[:, :units].astype(BF16)
        up_ref[0, chunk * width : (chunk + 1) * width] = raw[:, units:].astype(BF16)


def whole_vmem(count):
    return [pl.BlockSpec(memory_space=pltpu.VMEM)] * count


def kernel_body(tokens, routes, gate_weight, up_weight, hidden_grad, clip_limit):
    chunks = lax.axis_size("expert")
    d_count = lax.axis_size("dp")
    experts, model_width, hidden_units = gate_weight.shape
    block_rows, width = tokens.shape
    capacity = hidden_grad.shape[2]
    slots = d_count * capacity
    all_units = chunks * d_count
    token_rows = d_count * block_rows
    limit = jnp.broadcast_to(jnp.pad(clip_limit, (0, 8 - experts))[:, None], (8, 128))
    dma = pltpu.SemaphoreType.DMA
    hidden, act, rows, scale, totals = pl.pallas_call(
        expert_kernel,
        out_shape=[
            jax.ShapeDtypeStruct((experts, slots, hidden_units), BF16),
            jax.ShapeDtypeStruct((experts, slots, 2 * hidden_units), BF16),
            jax.ShapeDtypeStruct((chunks, experts * slots, width), BF16),
            jax.ShapeDtypeStruct((experts, 1, 128), F32),
            jax.ShapeDtypeStruct((Z_COUNT, block_rows, width), BF16),
        ],
        in_specs=whole_vmem(4) + [pl.BlockSpec(memory_space=pl.ANY)] * 2,
        out_specs=whole_vmem(5),
        scratch_shapes=[
            pltpu.VMEM((all_units, block_rows, width), BF16),
            pltpu.VMEM((all_units, block_rows, width), BF16),
            pltpu.VMEM((experts, model_width, hidden_units), BF16),
            pltpu.VMEM((experts, model_width, hidden_units), BF16),
            pltpu.VMEM((experts * slots, token_rows), BF16),
            pltpu.VMEM((experts, slots, 2 * hidden_units), F32),
            pltpu.VMEM((experts, slots, slots), F32),
            pltpu.VMEM((token_rows, experts * slots), BF16),
            pltpu.VMEM((16, block_rows, width), BF16),
            pltpu.VMEM((28, block_rows, width), BF16),
            pltpu.VMEM((8, 128), F32),
            pltpu.VMEM((3, 8, 128), F32),
            dma((2, chunks)), dma((31,)), dma((32,)), dma((28,)), dma((28,)), dma((3,)), dma((3,)),
        ],
        compiler_params=pltpu.CompilerParams(
            collective_id=0, has_side_effects=True, vmem_limit_bytes=VMEM_LIMIT
        ),
        name="experts",
    )(
        tokens, routes.T, hidden_grad.reshape(experts, slots, hidden_units), limit,
        gate_weight, up_weight,
    )
    arrived = []
    for j in range(1, Z_COUNT):
        pairs = [(i, 2 * ((i // 2) ^ j) + i % 2) for i in range(chunks)]
        arrived.append(lax.ppermute(totals[j], "expert", pairs))
    grad_gate, grad_up, hidden = weight_grads(rows, act, hidden, scale, gate_weight.shape)
    token_grad = totals[0].astype(F32)
    for block in arrived:
        token_grad = token_grad + block.astype(F32)
    return (hidden.reshape(hidden_grad.shape), grad_gate, grad_up, token_grad.astype(BF16))


def weight_grads(rows, act, hidden, scale, shape):
    experts, model_width, hidden_units = shape
    chunks, _, width = rows.shape
    slots = act.shape[1]
    halves = 2
    count = chunks // halves
    out_block = pl.BlockSpec((1, count * width, hidden_units), lambda e, h: (e, h, 0))
    hidden_block = pl.BlockSpec((1, slots, hidden_units), lambda e, h: (e, 0, 0))
    return pl.pallas_call(
        functools.partial(weight_grad_kernel, count),
        grid=(experts, halves),
        out_shape=[jax.ShapeDtypeStruct(shape, BF16)] * 2
        + [jax.ShapeDtypeStruct(hidden.shape, BF16)],
        in_specs=[
            pl.BlockSpec((1, 1, 128), lambda e, h: (e, 0, 0)),
            pl.BlockSpec((count, slots, width), lambda e, h: (h, e, 0)),
            pl.BlockSpec((1, slots, 2 * hidden_units), lambda e, h: (e, 0, 0)),
            hidden_block,
        ],
        out_specs=[out_block, out_block, hidden_block],
        cost_estimate=pl.CostEstimate(
            flops=4 * experts * slots * model_width * hidden_units,
            bytes_accessed=4 * experts * model_width * hidden_units + 2 * rows.size,
            transcendentals=0,
        ),
        compiler_params=pltpu.CompilerParams(vmem_limit_bytes=VMEM_LIMIT),
        name="weight_grads",
    )(scale, rows, act, hidden)


def solution(mesh):
    placed = (
        P("dp", "expert"),
        P(),
        P("expert", None, "dp"),
        P("expert", None, "dp"),
        P("expert", None, None, "dp"),
        P("expert"),
    )
    fits = mesh.shape["dp"] == 4 and mesh.shape["expert"] == 2 * Z_COUNT
    return jax.shard_map(
        kernel_body if fits else plain_body,
        mesh=mesh,
        in_specs=placed,
        out_specs=(
            P("expert", None, None, "dp"),
            P("expert", None, "dp"),
            P("expert", None, "dp"),
            P("dp", "expert"),
        ),
        check_vma=False,
    )
```

```python
import functools

import jax
import jax.numpy as jnp
from jax import lax
from jax.experimental import pallas as pl
from jax.experimental.pallas import tpu as pltpu
from jax.sharding import PartitionSpec as P


def slot_tables(block_routes, experts, capacity, top_count):
    flat_routes = block_routes.reshape(-1)
    expert_ids = jnp.arange(experts, dtype=jnp.int32)
    onehot = (flat_routes[:, None] == expert_ids[None, :]).astype(jnp.int32)
    before = jnp.cumsum(onehot, axis=0) - onehot
    slot_ranks = jnp.sum(before * onehot, axis=1)
    owner_token = jnp.arange(flat_routes.shape[0], dtype=jnp.int32) // top_count
    token_of = (
        jnp.zeros((experts, capacity), jnp.int32).at[flat_routes, slot_ranks].set(owner_token)
    )
    occupied = jnp.zeros((experts, capacity), jnp.bool_).at[flat_routes, slot_ranks].set(True)
    return (slot_ranks.reshape(block_routes.shape), token_of, occupied)


def expert_math(row_block, grad_block, gate_w, up_w):
    gate_pre = jnp.dot(row_block, gate_w, preferred_element_type=jnp.float32)
    up_pre = jnp.dot(row_block, up_w, preferred_element_type=jnp.float32)
    sigma_gate = jax.nn.sigmoid(gate_pre)
    hidden_rows = (gate_pre * sigma_gate * up_pre).astype(jnp.bfloat16)
    grad_float = grad_block.astype(jnp.float32)
    up_act = (grad_float * gate_pre * sigma_gate).astype(jnp.bfloat16)
    gate_act = (grad_float * up_pre * sigma_gate * (1.0 + gate_pre * (1.0 - sigma_gate))).astype(
        jnp.bfloat16
    )
    over_rows = (((0,), (0,)), ((), ()))
    over_units = (((1,), (1,)), ((), ()))
    raw_gate = lax.dot_general(row_block, gate_act, over_rows, preferred_element_type=jnp.float32)
    raw_up = lax.dot_general(row_block, up_act, over_rows, preferred_element_type=jnp.float32)
    partial_value = lax.dot_general(
        gate_act, gate_w, over_units, preferred_element_type=jnp.float32
    )
    partial_value = partial_value + lax.dot_general(
        up_act, up_w, over_units, preferred_element_type=jnp.float32
    )
    return (hidden_rows, raw_gate, raw_up, partial_value)


def plain_body(tokens, routes, gate_weight, up_weight, hidden_grad, clip_limit):
    dp_count = lax.axis_size("dp")
    expert_count = lax.axis_size("expert")
    local_experts = gate_weight.shape[0]
    experts = local_experts * expert_count
    capacity = hidden_grad.shape[2]
    hidden_units = gate_weight.shape[2]
    model_width = gate_weight.shape[1]
    top_count = routes.shape[1]
    tok_rows = tokens.shape[0]
    dp_index = lax.axis_index("dp")
    blocks = routes.reshape(dp_count, tok_rows, top_count)
    own_routes = lax.dynamic_index_in_dim(blocks, dp_index, 0, keepdims=False)
    slot_ranks, token_of, occupied = slot_tables(own_routes, experts, capacity, top_count)
    outgoing = jnp.where(occupied[:, :, None], tokens[token_of], jnp.zeros((), tokens.dtype))[
        :, None
    ]
    arrived = lax.all_to_all(outgoing, "expert", split_axis=0, concat_axis=3, tiled=True)
    gathered = lax.all_gather(arrived, "dp", axis=1, tiled=True)
    hidden_list = []
    gate_list = []
    up_list = []
    partial_list = []
    squares = []
    for expert_item in range(local_experts):
        row_block = gathered[expert_item].reshape(dp_count * capacity, model_width)
        grad_block = hidden_grad[expert_item].reshape(dp_count * capacity, hidden_units)
        hidden_rows, raw_gate, raw_up, partial_value = expert_math(
            row_block, grad_block, gate_weight[expert_item], up_weight[expert_item]
        )
        hidden_list.append(hidden_rows.reshape(dp_count, capacity, hidden_units))
        gate_list.append(raw_gate)
        up_list.append(raw_up)
        partial_list.append(partial_value.reshape(dp_count, capacity, model_width))
        squares.append(jnp.sum(raw_gate * raw_gate) + jnp.sum(raw_up * raw_up))
    totals = lax.psum(jnp.stack(squares), "dp")
    root_mean = jnp.sqrt(totals / (2.0 * model_width * hidden_units * dp_count) + 1e-06)
    clip_scale = jnp.minimum(1.0, clip_limit / root_mean)
    grad_gate = (clip_scale[:, None, None] * jnp.stack(gate_list)).astype(jnp.bfloat16)
    grad_up = (clip_scale[:, None, None] * jnp.stack(up_list)).astype(jnp.bfloat16)
    hidden = jnp.stack(hidden_list)
    partials = jnp.stack(partial_list)
    own_sums = lax.psum_scatter(
        partials.astype(jnp.bfloat16), "dp", scatter_dimension=1, tiled=True
    ).astype(jnp.float32)
    returned = lax.all_to_all(
        own_sums.astype(jnp.bfloat16), "expert", split_axis=3, concat_axis=0, tiled=True
    ).astype(own_sums.dtype)
    flat_back = returned.reshape(experts * capacity, -1)
    picked = flat_back[own_routes * capacity + slot_ranks]
    token_grad = jnp.sum(picked, axis=1).astype(jnp.bfloat16)
    return (hidden, grad_gate, grad_up, token_grad)


VMEM_LIMIT = 60 * 1024 * 1024
F32 = jnp.float32
BF16 = jnp.bfloat16
Z_COUNT = 4


def flip(bit, by):
    return bit + by - 2 * bit * by


class Place:
    def __init__(self):
        self.dp = lax.axis_index("dp")
        self.ex = lax.axis_index("expert")
        self.y, self.k = self.dp // 2, self.dp % 2
        self.z, self.x = self.ex // 2, self.ex % 2

    def z_at(self, j):
        return 2 * flip(self.z // 2, j // 2) + flip(self.z % 2, j % 2)

    def unit(self, core, s, f, j):
        xx = flip(self.x, f * (1 - core) + s * core)
        yy = flip(self.y, s * (1 - core) + f * core)
        return (2 * self.z_at(j) + xx) * 4 + 2 * yy + core

    def sibling(self):
        return (2 * self.y + 1 - self.k, self.ex)

    def second(self):
        return (2 * flip(self.y, 1 - self.k) + self.k, 2 * self.z + flip(self.x, self.k))

    def first(self):
        return (2 * flip(self.y, self.k) + self.k, 2 * self.z + flip(self.x, 1 - self.k))

    def along_z(self, j):
        return (self.dp, 2 * self.z_at(j) + self.x)

    def across(self):
        return (3 - self.dp, self.ex)

    def other_y(self):
        return (2 * (1 - self.y) + self.k, self.ex)

    def partners(self):
        others = [self.sibling(), self.first(), self.second(), self.across()]
        return others + [self.along_z(j) for j in range(1, Z_COUNT)]

    def greet(self):
        barrier = pltpu.get_barrier_semaphore()
        for partner in self.partners():
            pl.semaphore_signal(
                barrier, inc=1, device_id=partner, device_id_type=pl.DeviceIdType.MESH
            )

    def enter(self):
        pl.semaphore_wait(pltpu.get_barrier_semaphore(), len(self.partners()))


def label(s, f, j):
    return s * 8 + f * 4 + j


class Gather:
    def __init__(self, place, units, send_sem, recv_sem):
        self.place, self.units = place, units
        self.send_sem, self.recv_sem = send_sem, recv_sem

    def copy(self, unit, device, send_index, recv_index):
        return pltpu.make_async_remote_copy(
            src_ref=self.units.at[unit],
            dst_ref=self.units.at[unit],
            send_sem=self.send_sem.at[send_index],
            recv_sem=self.recv_sem.at[recv_index],
            device_id=device,
            device_id_type=pl.DeviceIdType.MESH,
        )

    def arrive(self, unit, recv_index):
        self.copy(unit, self.place.sibling(), 0, recv_index).wait_recv()

    def forward(self, s, f, j, own=False):
        place = self.place
        unit = place.unit(place.k, s, f, j)
        if not own:
            self.arrive(unit, label(s, f, j))
        if s == 0:
            self.copy(unit, place.second(), f * 4 + j, label(1, f, j)).start()
        if s == 0 and f == 0:
            self.copy(unit, place.first(), 8 + j, label(0, 1, j)).start()
        if own:
            for to in range(1, Z_COUNT):
                self.copy(unit, place.along_z(to), 11 + to, label(0, 0, to)).start()
        held = label(s, f, j)
        self.copy(unit, place.sibling(), 15 + held, 16 + held).start()

    def from_sibling(self, xf, yf, j):
        core = 1 - self.place.k
        s, f = xf * core + yf * (1 - core), xf * (1 - core) + yf * core
        self.arrive(self.place.unit(core, s, f, j), 16 + label(s, f, j))

    def finish(self):
        for i in range(31):
            self.copy(self.place.unit(self.place.k, 0, 0, 0), self.place.sibling(), i, 0).wait_send()


def one_hot_rows(routes, first_expert, experts, capacity):
    tokens = routes.shape[1]
    masks = [
        jnp.sum((routes == first_expert + e).astype(F32), axis=0, keepdims=True)
        for e in range(experts)
    ]
    mask = jnp.concatenate(masks + [jnp.zeros((8 - experts, tokens), F32)], axis=0)
    earlier = lax.broadcasted_iota(jnp.int32, (tokens, tokens), 0)
    later = lax.broadcasted_iota(jnp.int32, (tokens, tokens), 1)
    counted = jnp.where(earlier < later, 1.0, 0.0).astype(BF16)
    rank = jnp.dot(mask.astype(BF16), counted, preferred_element_type=F32)
    slot = jnp.where(mask > 0.5, rank, -1.0)
    rows = lax.broadcasted_iota(jnp.int32, (capacity, tokens), 0).astype(F32)
    return jnp.concatenate(
        [jnp.where(rows == slot[e : e + 1], 1.0, 0.0).astype(BF16) for e in range(experts)], axis=0
    )


OVER_LANES = (((1,), (1,)), ((), ()))
OVER_ROWS = (((0,), (0,)), ((), ()))


def dot(a, b, dims=(((1,), (0,)), ((), ()))):
    return lax.dot_general(a, b, dims, preferred_element_type=F32)


def start_weights(gate_hbm, up_hbm, gate_v, up_v, weight_sem, chunk):
    width = gate_hbm.shape[1] // weight_sem.shape[1]
    rows = pl.ds(chunk * width, width)
    copies = [
        pltpu.make_async_copy(gate_hbm.at[:, rows], gate_v.at[:, rows], weight_sem.at[0, chunk]),
        pltpu.make_async_copy(up_hbm.at[:, rows], up_v.at[:, rows], weight_sem.at[1, chunk]),
    ]
    return copies


def activate(e, acc_ref, grad_ref, hidden_ref, act_ref):
    units = grad_ref.shape[2]
    gate_pre = acc_ref[e, :, :units]
    up_pre = acc_ref[e, :, units:]
    sigma = jax.nn.sigmoid(gate_pre)
    grad = grad_ref[e].astype(F32)
    hidden_ref[e] = (gate_pre * sigma * up_pre).astype(BF16)
    act_ref[e, :, units:] = (grad * gate_pre * sigma).astype(BF16)
    act_ref[e, :, :units] = (grad * up_pre * sigma * (1.0 + gate_pre * (1.0 - sigma))).astype(BF16)


class Scatter:
    def __init__(self, place, sums, work, buffers, send_sem, recv_sem):
        self.place, self.sums, self.work = place, sums, work
        self.buffers = buffers
        self.send_sem, self.recv_sem = send_sem, recv_sem

    def copy(self, src, slot, device):
        return pltpu.make_async_remote_copy(
            src_ref=src,
            dst_ref=self.buffers.at[slot],
            send_sem=self.send_sem.at[slot],
            recv_sem=self.recv_sem.at[slot],
            device_id=device,
            device_id_type=pl.DeviceIdType.MESH,
        )

    def take(self, slot):
        self.copy(self.buffers.at[slot], slot, self.place.sibling()).wait_recv()
        return self.buffers[slot].astype(F32)

    def to_sibling(self, xf, j):
        place = self.place
        core = 1 - place.k
        for yf in range(2):
            s, f = xf * core + yf * (1 - core), xf * (1 - core) + yf * core
            unit = place.unit(core, s, f, j)
            self.copy(self.sums.at[unit], label(s, f, j), place.sibling()).start()

    def collect(self, s, f, j):
        place = self.place
        total = self.sums[place.unit(place.k, s, f, j)].astype(F32)
        total = total + self.take(label(s, f, j))
        if s == 0:
            total = total + self.take(16 + f * 4 + j)
        if s == 0 and f == 0:
            total = total + self.take(24 + j)
        return total

    def pass_on(self, s, f, j):
        place = self.place
        held = label(s, f, j)
        self.work[held] = self.collect(s, f, j).astype(BF16)
        if s == 1:
            self.copy(self.work.at[held], 16 + f * 4 + j, place.second()).start()
        else:
            self.copy(self.work.at[held], 24 + j, place.first()).start()

    def finish(self):
        for slot in range(28):
            self.copy(self.buffers.at[slot], slot, self.place.sibling()).wait_send()


def expert_kernel(
    tokens_ref, routes_ref, grad_ref, limit_ref, gate_hbm, up_hbm,
    hidden_ref, act_ref, rows_ref, scale_ref, total_0, total_1, total_2, total_3,
    units_ref, sums_ref, gate_v, up_v, onehot_ref, acc_ref, gram_ref, back_ref,
    work, buffers, square_ref, square_buf,
    weight_sem, gather_send, gather_recv, scatter_send, scatter_recv, square_send, square_recv,
):
    experts, slots, units = grad_ref.shape
    chunks = rows_ref.shape[0]
    width = rows_ref.shape[2]
    d_count = units_ref.shape[0] // chunks
    block_rows = tokens_ref.shape[0]
    place = Place()
    total_refs = (total_0, total_1, total_2, total_3)

    def chunk_at(xf, j):
        return 2 * place.z_at(j) + flip(place.x, xf)

    def weights(chunk):
        return start_weights(gate_hbm, up_hbm, gate_v, up_v, weight_sem, chunk)

    for j in range(Z_COUNT):
        for xf in range(2):
            for copy in weights(chunk_at(xf, j)):
                copy.start()
    place.greet()
    units_ref[place.unit(place.k, 0, 0, 0)] = tokens_ref[...]
    capacity = slots // d_count
    first_expert = place.ex * experts
    onehots = []
    for d in range(d_count):
        routes = routes_ref[:, d * block_rows : (d + 1) * block_rows]
        onehots.append(one_hot_rows(routes, first_expert, experts, capacity))
        onehot_ref[d] = onehots[d]
    place.enter()
    gather = Gather(place, units_ref, gather_send, gather_recv)
    gather.forward(0, 0, 0, own=True)
    for d in range(d_count):
        back_ref[d] = onehots[d].T
    acc_ref[...] = jnp.zeros_like(acc_ref)
    gram_ref[...] = jnp.zeros_like(gram_ref)
    gather.forward(0, 1, 0)
    gather.forward(0, 0, 1)
    gather.forward(1, 0, 0)
    gather.forward(0, 1, 1)
    gather.forward(0, 0, 2)
    gather.forward(1, 1, 0)

    def multiply(xf, j):
        chunk = chunk_at(xf, j)
        gather.from_sibling(xf, 0, j)
        gather.from_sibling(xf, 1, j)
        for copy in weights(chunk):
            copy.wait()
        for d in range(d_count):
            found = dot(onehot_ref[d], units_ref[chunk * d_count + d]).astype(BF16)
            for e in range(experts):
                at = e * slots + d * capacity
                rows_ref[chunk, at : at + capacity] = found[e * capacity : (e + 1) * capacity]
        span = pl.ds(pl.multiple_of(chunk * width, 64), width)
        for e in range(experts):
            mine = rows_ref[chunk, e * slots : (e + 1) * slots]
            acc_ref[e, :, :units] += dot(mine, gate_v[e, span])
            acc_ref[e, :, units:] += dot(mine, up_v[e, span])
            gram_ref[e] += dot(mine, mine, OVER_LANES)

    def forward(j, carry):
        multiply(0, j)

        @pl.when(j == 0)
        def _():
            gather.forward(0, 0, 3)

        @pl.when(j < Z_COUNT - 2)
        def _():
            gather.forward(0, 1, j + 2)

        @pl.when(j < Z_COUNT - 1)
        def _():
            gather.forward(1, 0, j + 1)
            gather.forward(1, 1, j + 1)

        multiply(1, j)
        return carry

    lax.fori_loop(0, Z_COUNT, forward, 0)
    squares = []
    for e in range(experts):
        activate(e, acc_ref, grad_ref, hidden_ref, act_ref)
        act = act_ref[e]
        product = dot(act, act, OVER_LANES) * gram_ref[e]
        squares.append(jnp.sum(jnp.sum(product, axis=0, keepdims=True), axis=1, keepdims=True))
    squares.append(jnp.zeros((8 - experts, 1), F32))
    square_ref[...] = jnp.broadcast_to(jnp.concatenate(squares, axis=0), square_ref.shape)
    square_copies = []
    for i, other in enumerate([place.sibling(), place.other_y(), place.across()]):
        copy = pltpu.make_async_remote_copy(
            src_ref=square_ref,
            dst_ref=square_buf.at[i],
            send_sem=square_send.at[i],
            recv_sem=square_recv.at[i],
            device_id=other,
            device_id_type=pl.DeviceIdType.MESH,
        )
        copy.start()
        square_copies.append(copy)

    scatter = Scatter(place, sums_ref, work, buffers, scatter_send, scatter_recv)

    def divide(xf, j):
        chunk = chunk_at(xf, j)
        span = pl.ds(pl.multiple_of(chunk * width, 64), width)
        parts = []
        for e in range(experts):
            part = dot(act_ref[e, :, :units], gate_v[e, span], OVER_LANES)
            part = part + dot(act_ref[e, :, units:], up_v[e, span], OVER_LANES)
            parts.append(part.astype(BF16))
        for d in range(d_count):
            mine = [part[d * capacity : (d + 1) * capacity] for part in parts]
            total = dot(back_ref[d], jnp.concatenate(mine, axis=0))
            sums_ref[chunk * d_count + d] = total.astype(BF16)
        scatter.to_sibling(xf, j)

    def far(j):
        scatter.pass_on(1, 1, j)

        @pl.when(place.k == 1)
        def _():
            scatter.pass_on(1, 0, j)

    def near(j):
        @pl.when(place.k == 0)
        def _():
            scatter.pass_on(1, 0, j)

        scatter.pass_on(0, 1, j)

    def backward_far(i, carry):
        divide(1, (i + 1) % Z_COUNT)

        @pl.when(i > 0)
        def _():
            far(i)

        return carry

    def backward_near(i, carry):
        divide(0, (i + 1) % Z_COUNT)

        @pl.when(i > 0)
        def _():
            near(i)

        @pl.when(i == 0)
        def _():
            far(0)

        return carry

    lax.fori_loop(0, Z_COUNT, backward_far, 0)
    lax.fori_loop(0, Z_COUNT, backward_near, 0)
    near(0)
    total_squares = square_ref[...]
    for i, copy in enumerate(square_copies):
        copy.wait()
        total_squares = total_squares + square_buf[i]
    mean = total_squares / (2.0 * chunks * width * units * d_count)
    root_mean = jnp.sqrt(mean + 1e-06)
    for e in range(experts):
        scale_ref[e] = jnp.minimum(1.0, limit_ref[e] / root_mean[e : e + 1])
    for j in (1, 2, 3, 0):
        total_refs[j][...] = scatter.collect(0, 0, j).astype(BF16)
    gather.finish()
    scatter.finish()


def weight_grad_kernel(count, scale_ref, rows_ref, act_ref, hidden_ref, gate_ref, up_ref, out_ref):
    width = rows_ref.shape[2]
    units = gate_ref.shape[2]
    scale = scale_ref[0, 0:1, 0:1]
    out_ref[...] = hidden_ref[...]
    for chunk in range(count):
        turned = rows_ref[chunk].T
        for start in range(0, 2 * units, 256):
            raw = dot(turned, act_ref[0, :, start : start + 256]) * scale
            out, at = (gate_ref, start) if start < units else (up_ref, start - units)
            out[0, chunk * width : (chunk + 1) * width, at : at + 256] = raw.astype(BF16)


def whole_vmem(count):
    return [pl.BlockSpec(memory_space=pltpu.VMEM)] * count


def kernel_body(tokens, routes, gate_weight, up_weight, hidden_grad, clip_limit):
    chunks = lax.axis_size("expert")
    d_count = lax.axis_size("dp")
    experts, model_width, hidden_units = gate_weight.shape
    block_rows, width = tokens.shape
    capacity = hidden_grad.shape[2]
    slots = d_count * capacity
    all_units = chunks * d_count
    dma = pltpu.SemaphoreType.DMA
    hidden, act, rows, scale, *totals = pl.pallas_call(
        expert_kernel,
        out_shape=[
            jax.ShapeDtypeStruct((experts, slots, hidden_units), BF16),
            jax.ShapeDtypeStruct((experts, slots, 2 * hidden_units), BF16),
            jax.ShapeDtypeStruct((chunks, experts * slots, width), BF16),
            jax.ShapeDtypeStruct((experts, 1, 128), F32),
        ]
        + [jax.ShapeDtypeStruct((block_rows, width), BF16)] * Z_COUNT,
        in_specs=whole_vmem(3)
        + [pl.BlockSpec(memory_space=pltpu.SMEM)]
        + [pl.BlockSpec(memory_space=pl.ANY)] * 2,
        out_specs=whole_vmem(4 + Z_COUNT),
        scratch_shapes=[
            pltpu.VMEM((all_units, block_rows, width), BF16),
            pltpu.VMEM((all_units, block_rows, width), BF16),
            pltpu.VMEM((experts, model_width, hidden_units), BF16),
            pltpu.VMEM((experts, model_width, hidden_units), BF16),
            pltpu.VMEM((d_count, experts * capacity, block_rows), BF16),
            pltpu.VMEM((experts, slots, 2 * hidden_units), F32),
            pltpu.VMEM((experts, slots, slots), F32),
            pltpu.VMEM((d_count, block_rows, experts * capacity), BF16),
            pltpu.VMEM((16, block_rows, width), BF16),
            pltpu.VMEM((28, block_rows, width), BF16),
            pltpu.VMEM((8, 128), F32),
            pltpu.VMEM((3, 8, 128), F32),
            dma((2, chunks)), dma((31,)), dma((32,)), dma((28,)), dma((28,)), dma((3,)), dma((3,)),
        ],
        compiler_params=pltpu.CompilerParams(
            collective_id=0, has_side_effects=True, vmem_limit_bytes=VMEM_LIMIT
        ),
        name="experts",
    )(
        tokens, routes.T, hidden_grad.reshape(experts, slots, hidden_units), clip_limit,
        gate_weight, up_weight,
    )
    arrived = []
    for j in range(1, Z_COUNT):
        pairs = [(i, 2 * ((i // 2) ^ j) + i % 2) for i in range(chunks)]
        arrived.append(lax.ppermute(totals[j], "expert", pairs))
    grad_gate, grad_up, hidden = weight_grads(rows, act, hidden, scale, gate_weight.shape)
    token_grad = totals[0].astype(F32)
    for block in arrived:
        token_grad = token_grad + block.astype(F32)
    return (hidden.reshape(hidden_grad.shape), grad_gate, grad_up, token_grad.astype(BF16))


def weight_grads(rows, act, hidden, scale, shape):
    experts, model_width, hidden_units = shape
    chunks, _, width = rows.shape
    slots = act.shape[1]
    halves = 2
    count = chunks // halves
    out_block = pl.BlockSpec((1, count * width, hidden_units), lambda e, h: (e, h, 0))
    hidden_block = pl.BlockSpec((1, slots, hidden_units), lambda e, h: (e, 0, 0))
    return pl.pallas_call(
        functools.partial(weight_grad_kernel, count),
        grid=(experts, halves),
        out_shape=[jax.ShapeDtypeStruct(shape, BF16)] * 2
        + [jax.ShapeDtypeStruct(hidden.shape, BF16)],
        in_specs=[
            pl.BlockSpec((1, 1, 128), lambda e, h: (e, 0, 0)),
            pl.BlockSpec((count, slots, width), lambda e, h: (h, e, 0)),
            pl.BlockSpec((1, slots, 2 * hidden_units), lambda e, h: (e, 0, 0)),
            hidden_block,
        ],
        out_specs=[out_block, out_block, hidden_block],
        cost_estimate=pl.CostEstimate(
            flops=4 * experts * slots * model_width * hidden_units,
            bytes_accessed=4 * experts * model_width * hidden_units + 2 * rows.size,
            transcendentals=0,
        ),
        compiler_params=pltpu.CompilerParams(vmem_limit_bytes=VMEM_LIMIT),
        name="weight_grads",
    )(scale, rows, act, hidden)


def solution(mesh):
    placed = (
        P("dp", "expert"),
        P(),
        P("expert", None, "dp"),
        P("expert", None, "dp"),
        P("expert", None, None, "dp"),
        P("expert"),
    )
    fits = mesh.shape["dp"] == 4 and mesh.shape["expert"] == 2 * Z_COUNT
    return jax.shard_map(
        kernel_body if fits else plain_body,
        mesh=mesh,
        in_specs=placed,
        out_specs=(
            P("expert", None, None, "dp"),
            P("expert", None, "dp"),
            P("expert", None, "dp"),
            P("dp", "expert"),
        ),
        check_vma=False,
    )
```

```python
import functools

import jax
import jax.numpy as jnp
from jax import lax
from jax.experimental import pallas as pl
from jax.experimental.pallas import tpu as pltpu
from jax.sharding import PartitionSpec as P


def slot_tables(block_routes, experts, capacity, top_count):
    flat_routes = block_routes.reshape(-1)
    expert_ids = jnp.arange(experts, dtype=jnp.int32)
    onehot = (flat_routes[:, None] == expert_ids[None, :]).astype(jnp.int32)
    before = jnp.cumsum(onehot, axis=0) - onehot
    slot_ranks = jnp.sum(before * onehot, axis=1)
    owner_token = jnp.arange(flat_routes.shape[0], dtype=jnp.int32) // top_count
    token_of = (
        jnp.zeros((experts, capacity), jnp.int32).at[flat_routes, slot_ranks].set(owner_token)
    )
    occupied = jnp.zeros((experts, capacity), jnp.bool_).at[flat_routes, slot_ranks].set(True)
    return (slot_ranks.reshape(block_routes.shape), token_of, occupied)


def expert_math(row_block, grad_block, gate_w, up_w):
    gate_pre = jnp.dot(row_block, gate_w, preferred_element_type=jnp.float32)
    up_pre = jnp.dot(row_block, up_w, preferred_element_type=jnp.float32)
    sigma_gate = jax.nn.sigmoid(gate_pre)
    hidden_rows = (gate_pre * sigma_gate * up_pre).astype(jnp.bfloat16)
    grad_float = grad_block.astype(jnp.float32)
    up_act = (grad_float * gate_pre * sigma_gate).astype(jnp.bfloat16)
    gate_act = (grad_float * up_pre * sigma_gate * (1.0 + gate_pre * (1.0 - sigma_gate))).astype(
        jnp.bfloat16
    )
    over_rows = (((0,), (0,)), ((), ()))
    over_units = (((1,), (1,)), ((), ()))
    raw_gate = lax.dot_general(row_block, gate_act, over_rows, preferred_element_type=jnp.float32)
    raw_up = lax.dot_general(row_block, up_act, over_rows, preferred_element_type=jnp.float32)
    partial_value = lax.dot_general(
        gate_act, gate_w, over_units, preferred_element_type=jnp.float32
    )
    partial_value = partial_value + lax.dot_general(
        up_act, up_w, over_units, preferred_element_type=jnp.float32
    )
    return (hidden_rows, raw_gate, raw_up, partial_value)


def plain_body(tokens, routes, gate_weight, up_weight, hidden_grad, clip_limit):
    dp_count = lax.axis_size("dp")
    expert_count = lax.axis_size("expert")
    local_experts = gate_weight.shape[0]
    experts = local_experts * expert_count
    capacity = hidden_grad.shape[2]
    hidden_units = gate_weight.shape[2]
    model_width = gate_weight.shape[1]
    top_count = routes.shape[1]
    tok_rows = tokens.shape[0]
    dp_index = lax.axis_index("dp")
    blocks = routes.reshape(dp_count, tok_rows, top_count)
    own_routes = lax.dynamic_index_in_dim(blocks, dp_index, 0, keepdims=False)
    slot_ranks, token_of, occupied = slot_tables(own_routes, experts, capacity, top_count)
    outgoing = jnp.where(occupied[:, :, None], tokens[token_of], jnp.zeros((), tokens.dtype))[
        :, None
    ]
    arrived = lax.all_to_all(outgoing, "expert", split_axis=0, concat_axis=3, tiled=True)
    gathered = lax.all_gather(arrived, "dp", axis=1, tiled=True)
    hidden_list = []
    gate_list = []
    up_list = []
    partial_list = []
    squares = []
    for expert_item in range(local_experts):
        row_block = gathered[expert_item].reshape(dp_count * capacity, model_width)
        grad_block = hidden_grad[expert_item].reshape(dp_count * capacity, hidden_units)
        hidden_rows, raw_gate, raw_up, partial_value = expert_math(
            row_block, grad_block, gate_weight[expert_item], up_weight[expert_item]
        )
        hidden_list.append(hidden_rows.reshape(dp_count, capacity, hidden_units))
        gate_list.append(raw_gate)
        up_list.append(raw_up)
        partial_list.append(partial_value.reshape(dp_count, capacity, model_width))
        squares.append(jnp.sum(raw_gate * raw_gate) + jnp.sum(raw_up * raw_up))
    totals = lax.psum(jnp.stack(squares), "dp")
    root_mean = jnp.sqrt(totals / (2.0 * model_width * hidden_units * dp_count) + 1e-06)
    clip_scale = jnp.minimum(1.0, clip_limit / root_mean)
    grad_gate = (clip_scale[:, None, None] * jnp.stack(gate_list)).astype(jnp.bfloat16)
    grad_up = (clip_scale[:, None, None] * jnp.stack(up_list)).astype(jnp.bfloat16)
    hidden = jnp.stack(hidden_list)
    partials = jnp.stack(partial_list)
    own_sums = lax.psum_scatter(
        partials.astype(jnp.bfloat16), "dp", scatter_dimension=1, tiled=True
    ).astype(jnp.float32)
    returned = lax.all_to_all(
        own_sums.astype(jnp.bfloat16), "expert", split_axis=3, concat_axis=0, tiled=True
    ).astype(own_sums.dtype)
    flat_back = returned.reshape(experts * capacity, -1)
    picked = flat_back[own_routes * capacity + slot_ranks]
    token_grad = jnp.sum(picked, axis=1).astype(jnp.bfloat16)
    return (hidden, grad_gate, grad_up, token_grad)


VMEM_LIMIT = 60 * 1024 * 1024
F32 = jnp.float32
BF16 = jnp.bfloat16
Z_COUNT = 4


def flip(bit, by):
    return bit + by - 2 * bit * by


class Place:
    def __init__(self):
        self.dp = lax.axis_index("dp")
        self.ex = lax.axis_index("expert")
        self.y, self.k = self.dp // 2, self.dp % 2
        self.z, self.x = self.ex // 2, self.ex % 2

    def z_at(self, j):
        return 2 * flip(self.z // 2, j // 2) + flip(self.z % 2, j % 2)

    def unit(self, core, s, f, j):
        xx = flip(self.x, f * (1 - core) + s * core)
        yy = flip(self.y, s * (1 - core) + f * core)
        return (2 * self.z_at(j) + xx) * 4 + 2 * yy + core

    def sibling(self):
        return (2 * self.y + 1 - self.k, self.ex)

    def second(self):
        return (2 * flip(self.y, 1 - self.k) + self.k, 2 * self.z + flip(self.x, self.k))

    def first(self):
        return (2 * flip(self.y, self.k) + self.k, 2 * self.z + flip(self.x, 1 - self.k))

    def along_z(self, j):
        return (self.dp, 2 * self.z_at(j) + self.x)

    def across(self):
        return (3 - self.dp, self.ex)

    def other_y(self):
        return (2 * (1 - self.y) + self.k, self.ex)

    def partners(self):
        others = [self.sibling(), self.first(), self.second(), self.across()]
        return others + [self.along_z(j) for j in range(1, Z_COUNT)]

    def greet(self):
        barrier = pltpu.get_barrier_semaphore()
        for partner in self.partners():
            pl.semaphore_signal(
                barrier, inc=1, device_id=partner, device_id_type=pl.DeviceIdType.MESH
            )

    def enter(self):
        pl.semaphore_wait(pltpu.get_barrier_semaphore(), len(self.partners()))


def label(s, f, j):
    return s * 8 + f * 4 + j


class Gather:
    def __init__(self, place, units, send_sem, recv_sem):
        self.place, self.units = place, units
        self.send_sem, self.recv_sem = send_sem, recv_sem

    def copy(self, unit, device, send_index, recv_index):
        return pltpu.make_async_remote_copy(
            src_ref=self.units.at[unit],
            dst_ref=self.units.at[unit],
            send_sem=self.send_sem.at[send_index],
            recv_sem=self.recv_sem.at[recv_index],
            device_id=device,
            device_id_type=pl.DeviceIdType.MESH,
        )

    def arrive(self, unit, recv_index):
        self.copy(unit, self.place.sibling(), 0, recv_index).wait_recv()

    def forward(self, s, f, j, own=False):
        place = self.place
        unit = place.unit(place.k, s, f, j)
        if not own:
            self.arrive(unit, label(s, f, j))
        if s == 0:
            self.copy(unit, place.second(), f * 4 + j, label(1, f, j)).start()
        if s == 0 and f == 0:
            self.copy(unit, place.first(), 8 + j, label(0, 1, j)).start()
        if own:
            for to in range(1, Z_COUNT):
                self.copy(unit, place.along_z(to), 11 + to, label(0, 0, to)).start()
        held = label(s, f, j)
        self.copy(unit, place.sibling(), 15 + held, 16 + held).start()

    def from_sibling(self, xf, yf, j):
        core = 1 - self.place.k
        s, f = xf * core + yf * (1 - core), xf * (1 - core) + yf * core
        self.arrive(self.place.unit(core, s, f, j), 16 + label(s, f, j))

    def finish(self):
        for i in range(31):
            self.copy(self.place.unit(self.place.k, 0, 0, 0), self.place.sibling(), i, 0).wait_send()


def one_hot_rows(routes, first_expert, experts, capacity):
    tokens = routes.shape[1]
    masks = [
        jnp.sum((routes == first_expert + e).astype(F32), axis=0, keepdims=True)
        for e in range(experts)
    ]
    mask = jnp.concatenate(masks + [jnp.zeros((8 - experts, tokens), F32)], axis=0)
    earlier = lax.broadcasted_iota(jnp.int32, (tokens, tokens), 0)
    later = lax.broadcasted_iota(jnp.int32, (tokens, tokens), 1)
    counted = jnp.where(earlier < later, 1.0, 0.0).astype(BF16)
    rank = jnp.dot(mask.astype(BF16), counted, preferred_element_type=F32)
    slot = jnp.where(mask > 0.5, rank, -1.0)
    rows = lax.broadcasted_iota(jnp.int32, (capacity, tokens), 0).astype(F32)
    return jnp.concatenate(
        [jnp.where(rows == slot[e : e + 1], 1.0, 0.0).astype(BF16) for e in range(experts)], axis=0
    )


OVER_LANES = (((1,), (1,)), ((), ()))
OVER_ROWS = (((0,), (0,)), ((), ()))


def dot(a, b, dims=(((1,), (0,)), ((), ()))):
    return lax.dot_general(a, b, dims, preferred_element_type=F32)


def start_weights(gate_hbm, up_hbm, gate_v, up_v, weight_sem, chunk):
    width = gate_hbm.shape[1] // weight_sem.shape[1]
    rows = pl.ds(chunk * width, width)
    copies = [
        pltpu.make_async_copy(gate_hbm.at[:, rows], gate_v.at[:, rows], weight_sem.at[0, chunk]),
        pltpu.make_async_copy(up_hbm.at[:, rows], up_v.at[:, rows], weight_sem.at[1, chunk]),
    ]
    return copies


def activate(e, acc_ref, grad_ref, hidden_ref, act_ref):
    units = grad_ref.shape[2]
    gate_pre = acc_ref[e, :, :units]
    up_pre = acc_ref[e, :, units:]
    sigma = jax.nn.sigmoid(gate_pre)
    grad = grad_ref[e].astype(F32)
    hidden_ref[e] = (gate_pre * sigma * up_pre).astype(BF16)
    act_ref[e, :, units:] = (grad * gate_pre * sigma).astype(BF16)
    act_ref[e, :, :units] = (grad * up_pre * sigma * (1.0 + gate_pre * (1.0 - sigma))).astype(BF16)


class Scatter:
    def __init__(self, place, sums, work, buffers, send_sem, recv_sem):
        self.place, self.sums, self.work = place, sums, work
        self.buffers = buffers
        self.send_sem, self.recv_sem = send_sem, recv_sem

    def copy(self, src, slot, device):
        return pltpu.make_async_remote_copy(
            src_ref=src,
            dst_ref=self.buffers.at[slot],
            send_sem=self.send_sem.at[slot],
            recv_sem=self.recv_sem.at[slot],
            device_id=device,
            device_id_type=pl.DeviceIdType.MESH,
        )

    def take(self, slot):
        self.copy(self.buffers.at[slot], slot, self.place.sibling()).wait_recv()
        return self.buffers[slot].astype(F32)

    def to_sibling(self, xf, j):
        place = self.place
        core = 1 - place.k
        for yf in range(2):
            s, f = xf * core + yf * (1 - core), xf * (1 - core) + yf * core
            unit = place.unit(core, s, f, j)
            self.copy(self.sums.at[unit], label(s, f, j), place.sibling()).start()

    def collect(self, s, f, j):
        place = self.place
        total = self.sums[place.unit(place.k, s, f, j)].astype(F32)
        total = total + self.take(label(s, f, j))
        if s == 0:
            total = total + self.take(16 + f * 4 + j)
        if s == 0 and f == 0:
            total = total + self.take(24 + j)
        return total

    def pass_on(self, s, f, j):
        place = self.place
        held = label(s, f, j)
        self.work[held] = self.collect(s, f, j).astype(BF16)
        if s == 1:
            self.copy(self.work.at[held], 16 + f * 4 + j, place.second()).start()
        elif f == 1:
            self.copy(self.work.at[held], 24 + j, place.first()).start()
        else:
            self.copy(self.work.at[held], 27 + j, place.along_z(j)).start()

    def finish(self):
        for slot in range(31):
            self.copy(self.buffers.at[slot], slot, self.place.sibling()).wait_send()


def expert_kernel(
    tokens_ref, routes_ref, grad_ref, limit_ref, gate_hbm, up_hbm,
    hidden_ref, act_ref, rows_ref, scale_ref, token_ref,
    units_ref, sums_ref, gate_v, up_v, onehot_ref, acc_ref, gram_ref, back_ref,
    work, buffers, square_ref, square_buf,
    weight_sem, gather_send, gather_recv, scatter_send, scatter_recv, square_send, square_recv,
):
    experts, slots, units = grad_ref.shape
    chunks = rows_ref.shape[0]
    width = rows_ref.shape[2]
    d_count = units_ref.shape[0] // chunks
    block_rows = tokens_ref.shape[0]
    place = Place()

    def chunk_at(xf, j):
        return 2 * place.z_at(j) + flip(place.x, xf)

    def weights(chunk):
        return start_weights(gate_hbm, up_hbm, gate_v, up_v, weight_sem, chunk)

    for j in range(Z_COUNT):
        for xf in range(2):
            for copy in weights(chunk_at(xf, j)):
                copy.start()
    place.greet()
    units_ref[place.unit(place.k, 0, 0, 0)] = tokens_ref[...]
    capacity = slots // d_count
    first_expert = place.ex * experts
    onehots = []
    for d in range(d_count):
        routes = routes_ref[:, d * block_rows : (d + 1) * block_rows]
        onehots.append(one_hot_rows(routes, first_expert, experts, capacity))
        onehot_ref[d] = onehots[d]
    place.enter()
    gather = Gather(place, units_ref, gather_send, gather_recv)
    gather.forward(0, 0, 0, own=True)
    for d in range(d_count):
        back_ref[d] = onehots[d].T
    acc_ref[...] = jnp.zeros_like(acc_ref)
    gram_ref[...] = jnp.zeros_like(gram_ref)
    gather.forward(0, 1, 0)
    gather.forward(0, 0, 1)
    gather.forward(1, 0, 0)
    gather.forward(0, 1, 1)
    gather.forward(0, 0, 2)
    gather.forward(1, 1, 0)

    def multiply(xf, j):
        chunk = chunk_at(xf, j)
        gather.from_sibling(xf, 0, j)
        gather.from_sibling(xf, 1, j)
        for copy in weights(chunk):
            copy.wait()
        for d in range(d_count):
            found = dot(onehot_ref[d], units_ref[chunk * d_count + d]).astype(BF16)
            for e in range(experts):
                at = e * slots + d * capacity
                rows_ref[chunk, at : at + capacity] = found[e * capacity : (e + 1) * capacity]
        span = pl.ds(pl.multiple_of(chunk * width, 64), width)
        for e in range(experts):
            mine = rows_ref[chunk, e * slots : (e + 1) * slots]
            acc_ref[e, :, :units] += dot(mine, gate_v[e, span])
            acc_ref[e, :, units:] += dot(mine, up_v[e, span])
            gram_ref[e] += dot(mine, mine, OVER_LANES)

    def forward(j, carry):
        multiply(0, j)

        @pl.when(j == 0)
        def _():
            gather.forward(0, 0, 3)

        @pl.when(j < Z_COUNT - 2)
        def _():
            gather.forward(0, 1, j + 2)

        @pl.when(j < Z_COUNT - 1)
        def _():
            gather.forward(1, 0, j + 1)
            gather.forward(1, 1, j + 1)

        multiply(1, j)
        return carry

    lax.fori_loop(0, Z_COUNT, forward, 0)
    squares = []
    for e in range(experts):
        activate(e, acc_ref, grad_ref, hidden_ref, act_ref)
        act = act_ref[e]
        product = dot(act, act, OVER_LANES) * gram_ref[e]
        squares.append(jnp.sum(jnp.sum(product, axis=0, keepdims=True), axis=1, keepdims=True))
    squares.append(jnp.zeros((8 - experts, 1), F32))
    square_ref[...] = jnp.broadcast_to(jnp.concatenate(squares, axis=0), square_ref.shape)
    square_copies = []
    for i, other in enumerate([place.sibling(), place.other_y(), place.across()]):
        copy = pltpu.make_async_remote_copy(
            src_ref=square_ref,
            dst_ref=square_buf.at[i],
            send_sem=square_send.at[i],
            recv_sem=square_recv.at[i],
            device_id=other,
            device_id_type=pl.DeviceIdType.MESH,
        )
        copy.start()
        square_copies.append(copy)

    scatter = Scatter(place, sums_ref, work, buffers, scatter_send, scatter_recv)

    def divide(xf, j):
        chunk = chunk_at(xf, j)
        span = pl.ds(pl.multiple_of(chunk * width, 64), width)
        parts = []
        for e in range(experts):
            part = dot(act_ref[e, :, :units], gate_v[e, span], OVER_LANES)
            part = part + dot(act_ref[e, :, units:], up_v[e, span], OVER_LANES)
            parts.append(part.astype(BF16))
        for d in range(d_count):
            mine = [part[d * capacity : (d + 1) * capacity] for part in parts]
            total = dot(back_ref[d], jnp.concatenate(mine, axis=0))
            sums_ref[chunk * d_count + d] = total.astype(BF16)
        scatter.to_sibling(xf, j)

    def far(j):
        scatter.pass_on(1, 1, j)

        @pl.when(place.k == 1)
        def _():
            scatter.pass_on(1, 0, j)

    def near(j):
        @pl.when(place.k == 0)
        def _():
            scatter.pass_on(1, 0, j)

        scatter.pass_on(0, 1, j)

    def backward_far(i, carry):
        divide(1, (i + 1) % Z_COUNT)

        @pl.when(i > 0)
        def _():
            far(i)

        return carry

    def backward_near(i, carry):
        divide(0, (i + 1) % Z_COUNT)

        @pl.when(i > 0)
        def _():
            near(i)

        @pl.when(i == 0)
        def _():
            far(0)

        return carry

    lax.fori_loop(0, Z_COUNT, backward_far, 0)
    lax.fori_loop(0, Z_COUNT, backward_near, 0)
    near(0)
    for j in range(1, Z_COUNT):
        scatter.pass_on(0, 0, j)
    total_squares = square_ref[...]
    for i, copy in enumerate(square_copies):
        copy.wait()
        total_squares = total_squares + square_buf[i]
    mean = total_squares / (2.0 * chunks * width * units * d_count)
    root_mean = jnp.sqrt(mean + 1e-06)
    for e in range(experts):
        scale_ref[e] = jnp.minimum(1.0, limit_ref[e] / root_mean[e : e + 1])
    total = scatter.collect(0, 0, 0)
    for j in range(1, Z_COUNT):
        total = total + scatter.take(27 + j)
    token_ref[...] = total.astype(BF16)
    gather.finish()
    scatter.finish()


def weight_grad_kernel(
    count, scale_ref, rows_ref, act_ref, hidden_ref, token_ref,
    gate_ref, up_ref, hidden_out, token_out,
):
    width = rows_ref.shape[2]
    units = gate_ref.shape[2]
    scale = scale_ref[0, 0:1, 0:1]
    hidden_out[...] = hidden_ref[...]
    token_out[...] = token_ref[...]
    for chunk in range(count):
        turned = rows_ref[chunk].T
        for start in range(0, 2 * units, 256):
            raw = dot(turned, act_ref[0, :, start : start + 256]) * scale
            out, at = (gate_ref, start) if start < units else (up_ref, start - units)
            out[0, chunk * width : (chunk + 1) * width, at : at + 256] = raw.astype(BF16)


def whole_vmem(count):
    return [pl.BlockSpec(memory_space=pltpu.VMEM)] * count


def kernel_body(tokens, routes, gate_weight, up_weight, hidden_grad, clip_limit):
    chunks = lax.axis_size("expert")
    d_count = lax.axis_size("dp")
    experts, model_width, hidden_units = gate_weight.shape
    block_rows, width = tokens.shape
    capacity = hidden_grad.shape[2]
    slots = d_count * capacity
    all_units = chunks * d_count
    dma = pltpu.SemaphoreType.DMA
    hidden, act, rows, scale, token_grad = pl.pallas_call(
        expert_kernel,
        out_shape=[
            jax.ShapeDtypeStruct((experts, slots, hidden_units), BF16),
            jax.ShapeDtypeStruct((experts, slots, 2 * hidden_units), BF16),
            jax.ShapeDtypeStruct((chunks, experts * slots, width), BF16),
            jax.ShapeDtypeStruct((experts, 1, 128), F32),
            jax.ShapeDtypeStruct((block_rows, width), BF16),
        ],
        in_specs=whole_vmem(3)
        + [pl.BlockSpec(memory_space=pltpu.SMEM)]
        + [pl.BlockSpec(memory_space=pl.ANY)] * 2,
        out_specs=whole_vmem(5),
        scratch_shapes=[
            pltpu.VMEM((all_units, block_rows, width), BF16),
            pltpu.VMEM((all_units, block_rows, width), BF16),
            pltpu.VMEM((experts, model_width, hidden_units), BF16),
            pltpu.VMEM((experts, model_width, hidden_units), BF16),
            pltpu.VMEM((d_count, experts * capacity, block_rows), BF16),
            pltpu.VMEM((experts, slots, 2 * hidden_units), F32),
            pltpu.VMEM((experts, slots, slots), F32),
            pltpu.VMEM((d_count, block_rows, experts * capacity), BF16),
            pltpu.VMEM((16, block_rows, width), BF16),
            pltpu.VMEM((31, block_rows, width), BF16),
            pltpu.VMEM((8, 128), F32),
            pltpu.VMEM((3, 8, 128), F32),
            dma((2, chunks)), dma((31,)), dma((32,)), dma((31,)), dma((31,)), dma((3,)), dma((3,)),
        ],
        compiler_params=pltpu.CompilerParams(
            collective_id=0, has_side_effects=True, vmem_limit_bytes=VMEM_LIMIT
        ),
        name="experts",
    )(
        tokens, routes.T, hidden_grad.reshape(experts, slots, hidden_units), clip_limit,
        gate_weight, up_weight,
    )
    grad_gate, grad_up, hidden, token_grad = weight_grads(
        rows, act, hidden, token_grad, scale, gate_weight.shape
    )
    return (hidden.reshape(hidden_grad.shape), grad_gate, grad_up, token_grad)


def weight_grads(rows, act, hidden, token_grad, scale, shape):
    experts, model_width, hidden_units = shape
    chunks, _, width = rows.shape
    slots = act.shape[1]
    halves = 2
    count = chunks // halves
    out_block = pl.BlockSpec((1, count * width, hidden_units), lambda e, h: (e, h, 0))
    token_block = pl.BlockSpec(token_grad.shape, lambda e, h: (0, 0))
    hidden_block = pl.BlockSpec((1, slots, hidden_units), lambda e, h: (e, 0, 0))
    return pl.pallas_call(
        functools.partial(weight_grad_kernel, count),
        grid=(experts, halves),
        out_shape=[jax.ShapeDtypeStruct(shape, BF16)] * 2
        + [jax.ShapeDtypeStruct(hidden.shape, BF16), jax.ShapeDtypeStruct(token_grad.shape, BF16)],
        in_specs=[
            pl.BlockSpec((1, 1, 128), lambda e, h: (e, 0, 0)),
            pl.BlockSpec((count, slots, width), lambda e, h: (h, e, 0)),
            pl.BlockSpec((1, slots, 2 * hidden_units), lambda e, h: (e, 0, 0)),
            hidden_block,
            token_block,
        ],
        out_specs=[out_block, out_block, hidden_block, token_block],
        cost_estimate=pl.CostEstimate(
            flops=4 * experts * slots * model_width * hidden_units,
            bytes_accessed=4 * experts * model_width * hidden_units + 2 * rows.size,
            transcendentals=0,
        ),
        compiler_params=pltpu.CompilerParams(vmem_limit_bytes=VMEM_LIMIT),
        name="weight_grads",
    )(scale, rows, act, hidden, token_grad)


def solution(mesh):
    placed = (
        P("dp", "expert"),
        P(),
        P("expert", None, "dp"),
        P("expert", None, "dp"),
        P("expert", None, None, "dp"),
        P("expert"),
    )
    fits = mesh.shape["dp"] == 4 and mesh.shape["expert"] == 2 * Z_COUNT
    return jax.shard_map(
        kernel_body if fits else plain_body,
        mesh=mesh,
        in_specs=placed,
        out_specs=(
            P("expert", None, None, "dp"),
            P("expert", None, "dp"),
            P("expert", None, "dp"),
            P("dp", "expert"),
        ),
        check_vma=False,
    )
```
